128 devices in a mesh: region: 4 (over z), tile: 32 (over y, x, core).
Axes of the slice: x: 4, y: 4, z: 4, core: 2. Of those that a mesh axis runs over, the one named last changes fastest.
Arguments:
- jacobian: bfloat16 [40, 30, 262144], P(None, None, ('region', 'tile')), may hold values from -1 to 1
- misfit: float32 [40, 262144], P(None, ('region', 'tile'))
- model: float32 [30, 262144], P(None, ('region', 'tile')), may hold values from -0.15 to 0.15
- vertical_weight: float32 [29, 262144], P(None, ('region', 'tile')), may hold values from 0.2 to 2
- lateral_weight: float32 [64, 4096], P('region', 'tile'), may hold values from 0.2 to 2
- send_order: int32 [262144], P(('region', 'tile')), may hold values from 0 to 2047, as said below
- line_id: int32 [262144], P(('region', 'tile')), may hold values from 0 to 511, as said below
Outputs:
- new_model: float32 [30, 262144], P(None, ('region', 'tile'))
- line_profile: float32 [512, 30], P(('region', 'tile'))
The draws below stay inside these ranges and needn't reach their ends.
Inputs may be any that keep to these rules, and one draw needn't show every extreme that they name: `send_order`: each aligned block of 2048 entries holds every number of 0 to 2047 once. `line_id`: let M = 128. Each aligned block b of 2048 entries is cut into 12 runs of one or more entries, in order; for k below 4, run k holds line b * 4 + k, run 4 + k holds line ((b - 1) mod M) * 4 + k, and run 2 * 4 + k holds line ((b - M / 2) mod M) * 4 + k.
All inputs are finite; a program needn't handle non-finite values.
Results may differ from the reference program's by a relative error of at most 0.0003.
Values sent between devices are 32-bit elements; how exact they have to be, the bound alone decides.
A program may use at most 64 MiB of HBM per device.

```python
import math
import jax
import jax.numpy as jnp
from jax import lax

NDATA = 40
LAYERS = 30
GX = 16
GY = 128
LINES_DEV = 4
ITERS = 2
SND_DEV = 2048
NS = 262144
NXG = 64
NYG = 4096
NGALL = 512
N_REGION = 4
N_TILE = 32


def draw_send_order(key, part):
    key = jax.random.fold_in(key, 11)
    keys = jax.random.split(key, NS // SND_DEV)

    def shuffle_block(block_key):
        return jax.random.permutation(block_key, SND_DEV)
    blocks = jax.vmap(shuffle_block)(keys)
    return blocks.reshape(NS).astype(jnp.int32)


def draw_line_id(key, part):
    key = jax.random.fold_in(key, 37)
    devices = NS // SND_DEV
    runs = 3 * LINES_DEV
    keys = jax.random.split(key, devices)
    positions = jnp.arange(SND_DEV, dtype=jnp.int32)

    def one_block(block_key, block):
        picked = jax.random.permutation(block_key, SND_DEV - 1)[:runs - 1].astype(jnp.int32) + 1
        run_index = jnp.sum((positions[:, None] >= picked[None, :]).astype(jnp.int32), axis=1)
        group = run_index // LINES_DEV
        within = run_index % LINES_DEV
        offset = jnp.where(group == 0, 0, jnp.where(group == 1, devices - 1, devices // 2)).astype(jnp.int32)
        source = (block + offset) % devices
        return (source * LINES_DEV + within).astype(jnp.int32)
    blocks = jax.vmap(one_block)(keys, jnp.arange(devices, dtype=jnp.int32))
    return blocks.reshape(NS).astype(jnp.int32)


def draw_misfit(key, part):
    key = jax.random.fold_in(key, 23)
    keys = jax.random.split(key, 3)
    gates = jnp.exp(jax.random.uniform(keys[0], (NDATA, 1), jnp.float32, math.log(0.4), math.log(4.0)))
    columns = jnp.exp(jax.random.uniform(keys[1], (1, NS), jnp.float32, math.log(0.4), math.log(4.0)))
    ramp = 1.0 + 2.0 * jnp.arange(NS, dtype=jnp.float32)[None, :] / (NS - 1)
    base = jax.random.normal(keys[2], (NDATA, NS), jnp.float32)
    return (base * gates * columns * ramp / 3.0).astype(jnp.float32)


def block_levels(stream_key, extent, cuts, smallest, largest):
    gain = 1.0
    for dim, blocks in cuts:
        heights = jax.random.uniform(jax.random.fold_in(jax.random.fold_in(stream_key, 6), dim), (blocks,), jnp.float32, smallest / len(cuts), largest / len(cuts))
        gain = gain * jnp.repeat(jnp.exp(heights), extent[dim] // blocks).reshape((-1,) + (1,) * (len(extent) - 1 - dim))
    return gain


def scatter_about(stream_key, extent, deviation, bound, pieces=(), held_as=jnp.bfloat16):
    drawn = jax.random.normal(stream_key, extent, jnp.float32) * deviation
    if len(pieces) > 0:
        drawn = block_levels(stream_key, extent, pieces, -0.22, 0.18) * drawn
    return jnp.clip(drawn, min=-bound, max=bound).astype(held_as)


def setup_inputs(seed: int = 0) -> dict:
    key_list = jax.random.split(jax.random.key(seed), 8)
    return {
        "jacobian": scatter_about(key_list[0], (NDATA, LAYERS, NS), NDATA ** -0.5, 1.0, ((2, 128),)),
        "misfit": draw_misfit(jax.random.fold_in(key_list[7], 71), 0),
        "model": jnp.clip(jax.random.uniform(key_list[2], (LAYERS, NS), jnp.float32, -0.15, 0.15) * block_levels(key_list[2], (LAYERS, NS), ((1, 128),), -0.4, 0.0), -0.15, 0.15),
        "vertical_weight": jnp.clip(jnp.exp(math.log(2.0) - 2.3025851 * jax.random.uniform(key_list[3], (LAYERS - 1, NS), jnp.float32) ** block_levels(key_list[3], (LAYERS - 1, NS), ((1, 128),), -0.2, 0.2)), 0.2, 2.0),
        "lateral_weight": jnp.clip(jnp.exp(math.log(2.0) - 2.3025851 * jax.random.uniform(key_list[4], (NXG, NYG), jnp.float32) ** block_levels(key_list[4], (NXG, NYG), ((0, 4), (1, 32)), -0.2, 0.2)), 0.2, 2.0),
        "send_order": draw_send_order(jax.random.fold_in(key_list[7], 71), 0),
        "line_id": draw_line_id(jax.random.fold_in(key_list[7], 71), 0),
    }


damping = 0.05
neighbours = ((1, 0, 1.0), (-1, 0, 1.0), (0, 1, 0.5), (0, -1, 0.5))


def to_tiles(vector, send_order):
    devices = N_REGION * N_TILE
    per_peer = SND_DEV // devices
    blocks = vector.reshape(LAYERS, devices, SND_DEV)
    orders = send_order.reshape(devices, SND_DEV)
    ordered = jnp.take_along_axis(blocks, orders[None], axis=2)
    ordered = ordered.reshape(LAYERS, devices, devices, per_peer).transpose(0, 2, 1, 3)
    ordered = ordered.reshape(LAYERS, N_REGION, N_TILE, GX, GY).transpose(0, 1, 3, 2, 4)
    return ordered.reshape(LAYERS, NXG, NYG)


def to_lines(grid_field, send_order):
    devices = N_REGION * N_TILE
    per_peer = SND_DEV // devices
    blocks = grid_field.reshape(LAYERS, N_REGION, GX, N_TILE, GY).transpose(0, 1, 3, 2, 4)
    blocks = blocks.reshape(LAYERS, devices, devices, per_peer).transpose(0, 2, 1, 3)
    blocks = blocks.reshape(LAYERS, devices, SND_DEV)
    inverse = jnp.argsort(send_order.reshape(devices, SND_DEV), axis=1).astype(jnp.int32)
    lines = jnp.take_along_axis(blocks, inverse[None], axis=2)
    return lines.reshape(LAYERS, NS)


def lateral_part(grid_field, lateral_weight):
    fields = jnp.pad(grid_field, ((0, 0), (1, 1), (1, 1)))
    conduct = jnp.pad(lateral_weight, 1)
    summed = jnp.zeros_like(grid_field)
    for step_row, step_col, factor in neighbours:
        beside = fields[:, 1 + step_row:1 + step_row + NXG, 1 + step_col:1 + step_col + NYG]
        beside_weight = conduct[1 + step_row:1 + step_row + NXG, 1 + step_col:1 + step_col + NYG]
        summed = summed + 0.5 * factor * (lateral_weight + beside_weight) * (grid_field - beside)
    return summed


def vertical_part(vector, vertical_weight):
    vertical_flux = vertical_weight * (vector[:-1] - vector[1:])
    return jnp.pad(vertical_flux, ((0, 1), (0, 0))) - jnp.pad(vertical_flux, ((1, 0), (0, 0)))


def blockwise(jacobian, vector, second):
    blocks_count = N_REGION * N_TILE

    def one_block(index):
        start = (index * SND_DEV).astype(jnp.int32)
        sens = lax.dynamic_slice_in_dim(jacobian, start, SND_DEV, 2).astype(jnp.float32)
        if second:
            piece = lax.dynamic_slice_in_dim(vector, start, SND_DEV, 1)
            predicted = jnp.sum(sens * piece[None], axis=1)
        else:
            predicted = lax.dynamic_slice_in_dim(vector, start, SND_DEV, 1)
        return jnp.sum(sens * predicted[:, None, :], axis=0)

    result = lax.map(one_block, jnp.arange(blocks_count, dtype=jnp.int32))
    return result.transpose(1, 0, 2).reshape(LAYERS, NS)


def reference(jacobian, misfit, model, vertical_weight, lateral_weight, send_order, line_id):
    def operate(vector):
        local_sum = blockwise(jacobian, vector, True) + vertical_part(vector, vertical_weight) + damping * vector
        return local_sum + to_lines(lateral_part(to_tiles(vector, send_order), lateral_weight), send_order)

    right_side = blockwise(jacobian, misfit, False)
    residual = right_side
    direction = right_side
    update = jnp.zeros_like(right_side)
    norm_old = jnp.sum(residual * residual)
    for iteration in range(ITERS):
        applied = operate(direction)
        step_length = norm_old / jnp.sum(direction * applied)
        update = update + step_length * direction
        residual = residual - step_length * applied
        norm_new = jnp.sum(residual * residual)
        direction = residual + (norm_new / norm_old) * direction
        norm_old = norm_new
    new_model = model + update
    line_sums = jax.ops.segment_sum(new_model.T, line_id, num_segments=NGALL)
    counts = jax.ops.segment_sum(jnp.ones((NS,), jnp.float32), line_id, num_segments=NGALL)
    return new_model, line_sums / counts[:, None]
```

```python
import jax
import jax.numpy as jnp
from jax import lax
from jax.experimental import pallas as pl
from jax.experimental.pallas import tpu as pltpu
from jax.sharding import PartitionSpec as P

LINES_DEV = 4
DAMPING = 0.05
GATES = 40
LAYERS = 30
PADDED = 32
SOUNDINGS = 2048
REGIONS = 4
TILES = 32
DEVICES = REGIONS * TILES
ROWS = 16
LANES = 128
BLOCKS = SOUNDINGS // LANES
CHUNKS = 4
MESH = pl.DeviceIdType.MESH
F32 = jnp.float32


def lane_iota(shape):
    return lax.broadcasted_iota(jnp.int32, shape, 1)


def row_iota(shape):
    return lax.broadcasted_iota(jnp.int32, shape, 0)


def total(values):
    return jnp.sum(values, keepdims=True)


def swap_pieces(parts):
    parts = list(parts)
    piece = lane_iota((8, LANES)) // 16
    for bit in (4, 2, 1):
        low = (piece & bit) == 0
        for first in range(8):
            if first & bit:
                continue
            a, b = parts[first], parts[first + bit]
            b_up = pltpu.roll(b, bit * 16, 1)
            a_down = pltpu.roll(a, LANES - bit * 16, 1)
            parts[first] = jnp.where(low, a, b_up)
            parts[first + bit] = jnp.where(low, a_down, b)
    return parts


def pick(source, group, index):
    low = index & (LANES - 1)
    high = index // LANES
    out = None
    for q in range(BLOCKS):
        block = source[group * 8 : group * 8 + 8, q * LANES : (q + 1) * LANES]
        taken = jnp.take_along_axis(block, low, axis=1, mode="promise_in_bounds")
        out = taken if out is None else jnp.where(high == q, taken, out)
    return out


def kernel(
    jac_hbm, misfit, model, vertical, lateral, order, order_s, line,
    new_model, profile,
    jac, fields, vert, send_a, recv_a, grid, coef, c_grid, d_grid, edge, side,
    send_b, recv_b, back, resid, inverse, onehot, extended,
    sums_s, sums_r, part_s, part_r,
    jac_sem, ring_s, ring_r, halo_s, halo_r, sums_ss, sums_rs,
):
    region = lax.axis_index("region")
    tile = lax.axis_index("tile")
    me = region * TILES + tile

    def place(device):
        return (device // TILES, device % TILES)

    def chunk_copy(chunk):
        columns = pl.ds(chunk * (SOUNDINGS // CHUNKS), SOUNDINGS // CHUNKS)
        return pltpu.make_async_copy(
            jac_hbm.at[:, :, columns], jac.at[:, :, columns], jac_sem.at[chunk]
        )

    for chunk in range(CHUNKS):
        chunk_copy(chunk).start()

    barrier = pltpu.get_barrier_semaphore()

    def greet(i, carry):
        pl.semaphore_signal(
            barrier, inc=1, device_id=place((me + i) % DEVICES), device_id_type=MESH
        )
        return carry

    lax.fori_loop(1, DEVICES, greet, 0)

    fields[...] = jnp.zeros_like(fields)
    vert[...] = jnp.zeros_like(vert)
    vert[0 : LAYERS - 1, :] = vertical[...]

    def local_part(block, sums):
        @pl.when(block % (BLOCKS // CHUNKS) == 0)
        def _():
            chunk_copy(block // (BLOCKS // CHUNKS)).wait()

        at = pl.ds(pl.multiple_of(block * LANES, LANES), LANES)

        def gather_gates(group, acc):
            data = misfit[pl.ds(pl.multiple_of(group * 8, 8), 8), at]
            for d in range(8):
                acc = acc + jac[group * 8 + d, :, at].astype(F32) * data[d : d + 1]
            return acc

        right = lax.fori_loop(0, GATES // 8, gather_gates, jnp.zeros((LAYERS, LANES), F32))

        def normal_gate(d, acc):
            sens = jac[d, :, at].astype(F32)
            return acc + sens * jnp.sum(sens * right, axis=0, keepdims=True)

        normal = lax.fori_loop(0, GATES, normal_gate, jnp.zeros((LAYERS, LANES), F32), unroll=8)
        fields[0:LAYERS, at] = right
        fields[PADDED : PADDED + LAYERS, at] = normal
        p = fields[0:PADDED, at]
        flux = vert[:, at] * (p - pltpu.roll(p, PADDED - 1, 0))
        applied = fields[PADDED:, at] + DAMPING * p + (flux - pltpu.roll(flux, 1, 0))
        fields[PADDED:, at] = applied
        return sums[0] + p * p, sums[1] + p * applied

    zero = jnp.zeros((PADDED, LANES), F32)
    square_sum, local_sum = lax.fori_loop(0, BLOCKS, local_part, (zero, zero))

    pl.semaphore_wait(barrier, DEVICES - 1)

    def send_block(i, carry):
        block = (me // 8 + i) % BLOCKS
        index = jnp.broadcast_to(order[pl.ds(block, 1), :], (8, LANES))
        for j, message in enumerate(swap_pieces([pick(fields, s, index) for s in range(8)])):
            send_a[block * 8 + j] = message
        for n in range(8):
            peer = block * 8 + (me + n) % 8

            def post():
                pltpu.make_async_remote_copy(
                    src_ref=send_a.at[peer],
                    dst_ref=recv_a.at[me],
                    send_sem=ring_s.at[0],
                    recv_sem=ring_r.at[0],
                    device_id=place(peer),
                    device_id_type=MESH,
                ).start()

            if n == 0:
                pl.when(i > 0)(post)
            else:
                post()
        return carry

    lax.fori_loop(0, BLOCKS, send_block, 0)
    recv_a[me] = send_a[me]

    places = row_iota((BLOCKS, LANES)) * LANES + lane_iota((BLOCKS, LANES))

    def invert(q, found):
        return jnp.where(places == order_s[q], q, found)

    inverse[...] = lax.fori_loop(
        0, SOUNDINGS, invert, jnp.zeros((BLOCKS, LANES), jnp.int32), unroll=16
    )

    run = row_iota((24, LANES))
    shift = jnp.where(run < 8, 0, jnp.where(run < 16, DEVICES - 1, DEVICES // 2))
    owner = (me + shift) & (DEVICES - 1)
    wanted = jnp.where((run & 7) < LINES_DEV, owner * LINES_DEV + (run & 7), -1)
    for block in range(BLOCKS):
        hit = line[block : block + 1, :] == wanted
        onehot[:, block * LANES : (block + 1) * LANES] = jnp.where(hit, 1.0, 0.0)
    extended[...] = jnp.ones_like(extended)
    extended[0:LAYERS, :] = model[...]

    def line_sums(slot, values):
        found = lax.dot_general(
            onehot[...], values, (((1,), (1,)), ((), ())),
            precision=lax.Precision.HIGHEST, preferred_element_type=F32,
        )
        for g in range(3):
            sums_s[g, slot, :, 0:PADDED] = found[8 * g : 8 * g + 8, :]

    sums_s[...] = jnp.zeros_like(sums_s)
    line_sums(0, extended[...])
    line_sums(1, fields[0:PADDED, :])

    def wait_ring(k, buffer, sem):
        whole = buffer.at[pl.ds(0, DEVICES - 1)]
        pltpu.make_async_copy(whole, whole, sem.at[k]).wait()

    wait_ring(0, recv_a, ring_r)
    wait_ring(0, send_a, ring_s)

    def place_row(i, carry):
        rows = swap_pieces([recv_a[i * 8 + j] for j in range(8)])
        for s in range(8):
            grid[i + 1, s * 8 : s * 8 + 8, :] = rows[s]
        grid[i + 1, LAYERS : LAYERS + 1, :] = lateral[pl.ds(i, 1), :]
        return carry

    lax.fori_loop(0, ROWS, place_row, 0)

    lane = lane_iota((PADDED, LANES))
    layer = row_iota((PADDED, LANES))

    def halo_copies(phase):
        ch = pl.ds(phase * PADDED, PADDED)
        above = ((region + REGIONS - 1) % REGIONS, tile)
        below = ((region + 1) % REGIONS, tile)
        left = (region, (tile + TILES - 1) % TILES)
        right = (region, (tile + 1) % TILES)
        pairs = (
            (grid.at[1, ch], grid.at[ROWS + 1, ch], above),
            (grid.at[ROWS, ch], grid.at[0, ch], below),
            (edge.at[phase, 0], side.at[phase, 1], left),
            (edge.at[phase, 1], side.at[phase, 0], right),
        )
        return [
            pltpu.make_async_remote_copy(
                src_ref=src, dst_ref=dst,
                send_sem=halo_s.at[phase, n], recv_sem=halo_r.at[phase, n],
                device_id=device, device_id_type=MESH,
            )
            for n, (src, dst, device) in enumerate(pairs)
        ]

    def halo_start(phase):
        first = phase * PADDED
        west = jnp.zeros((PADDED, LANES), F32)
        east = jnp.zeros((PADDED, LANES), F32)
        for i in range(ROWS):
            row = grid[i + 1, first : first + PADDED, :]
            west = jnp.where(lane == i, row if i == 0 else pltpu.roll(row, i, 1), west)
            east = jnp.where(lane == i, pltpu.roll(row, i + 1, 1), east)
        edge[phase, 0] = west
        edge[phase, 1] = east
        copies = halo_copies(phase)
        for copy in copies:
            copy.start()
        return copies

    def halo_finish(phase, copies):
        for copy in copies:
            copy.wait()
        ch = slice(phase * PADDED, (phase + 1) * PADDED)

        @pl.when(region == 0)
        def _():
            grid[0, ch, :] = jnp.zeros((PADDED, LANES), F32)

        @pl.when(region == REGIONS - 1)
        def _():
            grid[ROWS + 1, ch, :] = jnp.zeros((PADDED, LANES), F32)

        @pl.when(tile == 0)
        def _():
            side[phase, 0] = jnp.zeros((PADDED, LANES), F32)

        @pl.when(tile == TILES - 1)
        def _():
            side[phase, 1] = jnp.zeros((PADDED, LANES), F32)

    def lateral_row(i, phase, west, east):
        ch = slice(phase * PADDED, (phase + 1) * PADDED)
        here = grid[i + 1, ch, :]
        up, down = grid[i, ch, :], grid[i + 2, ch, :]
        west_of = jnp.where(lane == 0, west, pltpu.roll(here, 1, 1))
        east_of = jnp.where(lane == LANES - 1, east, pltpu.roll(here, LANES - 1, 1))
        if phase == 0:
            own = here[LAYERS : LAYERS + 1]
            for n, (other, factor) in enumerate(
                ((up, 0.5), (down, 0.5), (west_of, 0.25), (east_of, 0.25))
            ):
                coef[i, n : n + 1, :] = factor * (own + other[LAYERS : LAYERS + 1])
        return (
            coef[i, 0:1, :] * (here - up)
            + coef[i, 1:2, :] * (here - down)
            + coef[i, 2:3, :] * (here - west_of)
            + coef[i, 3:4, :] * (here - east_of)
        )

    def lateral_part(phase, out):
        def step(i, carry):
            west, east, dots = carry
            value = lateral_row(i, phase, west, east)
            out[i] = value
            here = grid[i + 1, 0:PADDED, :]
            return pltpu.roll(west, LANES - 1, 1), pltpu.roll(east, LANES - 1, 1), dots + here * value

        first = (side[phase, 0], pltpu.roll(side[phase, 1], LANES - 1, 1), zero)
        return lax.fori_loop(0, ROWS, step, first)[2]

    copies = halo_start(0)
    halo_finish(0, copies)
    lateral_sum = lateral_part(0, c_grid)

    inside = layer < LAYERS
    curve_part = total(jnp.where(inside, lateral_sum + local_sum, 0.0))
    square_part = total(square_sum)

    upper = row_iota((8, LANES)) < 4
    sublane = row_iota((8, LANES))

    def send_pair(i, carry):
        pair = (me // 16 + i) % (ROWS // 2)
        parts = [None] * 8
        for k in range(4):
            a = c_grid[2 * pair, 8 * k : 8 * k + 8, :]
            b = c_grid[2 * pair + 1, 8 * k : 8 * k + 8, :]
            if k == 3:
                a = jnp.where(sublane == 6, curve_part, jnp.where(sublane == 7, square_part, a))
                b = jnp.where(sublane == 6, curve_part, jnp.where(sublane == 7, square_part, b))
            parts[k] = jnp.where(upper, a, pltpu.roll(b, 4, 0))
            parts[k + 4] = jnp.where(upper, pltpu.roll(a, 4, 0), b)
        for j, message in enumerate(swap_pieces(parts)):
            send_b[pair * 16 + j] = message[0:4]
            send_b[pair * 16 + 8 + j] = message[4:8]
        for n in range(16):
            peer = pair * 16 + (me + n) % 16

            def post():
                pltpu.make_async_remote_copy(
                    src_ref=send_b.at[peer],
                    dst_ref=recv_b.at[me],
                    send_sem=ring_s.at[1],
                    recv_sem=ring_r.at[1],
                    device_id=place(peer),
                    device_id_type=MESH,
                ).start()

            if n == 0:
                pl.when(i > 0)(post)
            else:
                post()
        return carry

    lax.fori_loop(0, ROWS // 2, send_pair, 0)
    recv_b[me] = send_b[me]

    def add_image(i, carry):
        grid[i + 1, PADDED:, :] = grid[i + 1, PADDED:, :] + c_grid[i]
        return carry

    lax.fori_loop(0, ROWS, add_image, 0)
    copies = halo_start(1)
    halo_finish(1, copies)
    lateral_part(1, d_grid)

    wait_ring(1, recv_b, ring_r)
    wait_ring(1, send_b, ring_s)

    def unpack_pair(pair, carried):
        words = [
            jnp.concatenate([recv_b[pair * 16 + j], recv_b[pair * 16 + 8 + j]], axis=0)
            for j in range(8)
        ]
        parts = swap_pieces(words)
        even = pl.ds(pl.multiple_of(pair * 2 * LANES, LANES), LANES)
        odd = pl.ds(pl.multiple_of(pair * 2 * LANES + LANES, LANES), LANES)
        for k in range(4):
            a = jnp.where(upper, parts[k], pltpu.roll(parts[k + 4], 4, 0))
            b = jnp.where(upper, pltpu.roll(parts[k], 4, 0), parts[k + 4])
            back[8 * k : 8 * k + 8, even] = a
            back[8 * k : 8 * k + 8, odd] = b
            if k == 3:
                carried = carried + a + b
        return carried

    carried = lax.fori_loop(0, BLOCKS // 2, unpack_pair, jnp.zeros((8, LANES), F32))
    curve = total(carried[6:7]) * (1.0 / 16)
    square = total(carried[7:8]) * (1.0 / 16)
    step_0 = square / curve

    def second_part(block, sums):
        at = pl.ds(pl.multiple_of(block * LANES, LANES), LANES)
        index = jnp.broadcast_to(inverse[pl.ds(block, 1), :], (8, LANES))
        taken = jnp.concatenate([pick(back, k, index) for k in range(4)], axis=0)
        applied = fields[PADDED:, at] + jnp.where(inside, taken, 0.0)
        r = fields[0:PADDED, at] - step_0 * applied
        resid[:, at] = r
        drop = r - pltpu.roll(r, PADDED - 1, 0)
        trimmed = resid[0:LAYERS, at]

        def gate(d, acc):
            predicted = jnp.sum(jac[d, :, at].astype(F32) * trimmed, axis=0, keepdims=True)
            return acc + predicted * predicted

        gates = lax.fori_loop(0, GATES, gate, jnp.zeros((1, LANES), F32), unroll=8)
        return (
            sums[0] + r * r,
            sums[1] + r * applied,
            sums[2] + vert[:, at] * (drop * drop) + DAMPING * (r * r),
            sums[3] + gates,
        )

    r_square, r_image, r_curve, r_gates = lax.fori_loop(
        0, BLOCKS, second_part, (zero, zero, zero, jnp.zeros((1, LANES), F32))
    )

    def grid_curve(i, acc):
        r = grid[i + 1, 0:PADDED, :] - step_0 * grid[i + 1, PADDED:, :]
        return acc + r * (c_grid[i] - step_0 * d_grid[i])

    r_lateral = lax.fori_loop(0, ROWS, grid_curve, zero)
    r_curve = total(jnp.where(inside, r_curve + r_lateral, 0.0)) + total(r_gates)

    row = lane_iota((1, LANES))
    part = jnp.where(
        row == 0, total(r_square), jnp.where(row == 1, total(r_image), r_curve)
    )
    part_s[0] = part
    part_r[me] = part

    def share(i, carry):
        pltpu.make_async_remote_copy(
            src_ref=part_s.at[0],
            dst_ref=part_r.at[me],
            send_sem=ring_s.at[2],
            recv_sem=ring_r.at[2],
            device_id=place((me + i) % DEVICES),
            device_id_type=MESH,
        ).start()
        return carry

    lax.fori_loop(1, DEVICES, share, 0)

    line_sums(2, resid[...])
    sums_copies = []
    for g, offset in ((1, DEVICES - 1), (2, DEVICES // 2)):
        copy = pltpu.make_async_remote_copy(
            src_ref=sums_s.at[g],
            dst_ref=sums_r.at[g - 1],
            send_sem=sums_ss.at[g - 1],
            recv_sem=sums_rs.at[g - 1],
            device_id=place((me + offset) % DEVICES),
            device_id_type=MESH,
        )
        copy.start()
        sums_copies.append(copy)

    wait_ring(2, part_r, ring_r)
    wait_ring(2, part_r, ring_s)
    for copy in sums_copies:
        copy.wait()

    sums = jnp.sum(part_r[...], axis=0)
    square_1, cross, curve_r = sums[:, 0:1], sums[:, 1:2], sums[:, 2:3]
    beta = square_1 / square
    curve_1 = curve_r + 2.0 * beta * cross + beta * beta * curve
    step_1 = square_1 / curve_1
    weight = step_0 + step_1 * beta
    new_model[...] = (
        model[...] + weight * fields[0:LAYERS, :] + step_1 * resid[0:LAYERS, :]
    )
    sums = [sums_s[0, n] + sums_r[0, n] + sums_r[1, n] for n in range(3)]
    count = sums[0][:, LAYERS : LAYERS + 1]
    means = (sums[0] + weight * sums[1] + step_1 * sums[2]) / count
    profile[...] = means[0:LINES_DEV, 0:LAYERS]


def body(jacobian, misfit, model, vertical_weight, lateral_weight, send_order, line_id):
    vmem = pl.BlockSpec(memory_space=pltpu.VMEM)
    smem = pl.BlockSpec(memory_space=pltpu.SMEM)
    dma = pltpu.SemaphoreType.DMA
    return pl.pallas_call(
        kernel,
        out_shape=(
            jax.ShapeDtypeStruct((LAYERS, SOUNDINGS), F32),
            jax.ShapeDtypeStruct((LINES_DEV, LAYERS), F32),
        ),
        in_specs=[pl.BlockSpec(memory_space=pl.ANY), vmem, vmem, vmem, vmem, vmem, smem, vmem],
        out_specs=(vmem, vmem),
        scratch_shapes=[
            pltpu.VMEM((GATES, LAYERS, SOUNDINGS), jnp.bfloat16),
            pltpu.VMEM((2 * PADDED, SOUNDINGS), F32),
            pltpu.VMEM((PADDED, SOUNDINGS), F32),
            pltpu.VMEM((DEVICES, 8, LANES), F32),
            pltpu.VMEM((DEVICES, 8, LANES), F32),
            pltpu.VMEM((ROWS + 2, 2 * PADDED, LANES), F32),
            pltpu.VMEM((ROWS, 8, LANES), F32),
            pltpu.VMEM((ROWS, PADDED, LANES), F32),
            pltpu.VMEM((ROWS, PADDED, LANES), F32),
            pltpu.VMEM((2, 2, PADDED, LANES), F32),
            pltpu.VMEM((2, 2, PADDED, LANES), F32),
            pltpu.VMEM((DEVICES, 4, LANES), F32),
            pltpu.VMEM((DEVICES, 4, LANES), F32),
            pltpu.VMEM((PADDED, SOUNDINGS), F32),
            pltpu.VMEM((PADDED, SOUNDINGS), F32),
            pltpu.VMEM((BLOCKS, LANES), jnp.int32),
            pltpu.VMEM((24, SOUNDINGS), F32),
            pltpu.VMEM((PADDED, SOUNDINGS), F32),
            pltpu.VMEM((3, 3, 8, LANES), F32),
            pltpu.VMEM((2, 3, 8, LANES), F32),
            pltpu.VMEM((1, 1, LANES), F32),
            pltpu.VMEM((DEVICES, 1, LANES), F32),
            dma((CHUNKS,)),
            dma((3,)),
            dma((3,)),
            dma((2, 4)),
            dma((2, 4)),
            dma((2,)),
            dma((2,)),
        ],
        compiler_params=pltpu.CompilerParams(
            collective_id=0, has_side_effects=True, vmem_limit_bytes=48 * 1024 * 1024
        ),
    )(
        jacobian,
        misfit,
        model,
        vertical_weight,
        lateral_weight,
        send_order.reshape(BLOCKS, LANES),
        send_order,
        line_id.reshape(BLOCKS, LANES),
    )


def solution(mesh):
    in_specs = (
        P(None, None, ("region", "tile")),
        P(None, ("region", "tile")),
        P(None, ("region", "tile")),
        P(None, ("region", "tile")),
        P("region", "tile"),
        P(("region", "tile")),
        P(("region", "tile")),
    )
    out_specs = (P(None, ("region", "tile")), P(("region", "tile"), None))
    return jax.shard_map(body, mesh=mesh, in_specs=in_specs, out_specs=out_specs, check_vma=False)
```

```python
import jax
import jax.numpy as jnp
from jax import lax
from jax.experimental import pallas as pl
from jax.experimental.pallas import tpu as pltpu
from jax.sharding import PartitionSpec as P

LINES_DEV = 4
DAMPING = 0.05
GATES = 40
LAYERS = 30
PADDED = 32
SOUNDINGS = 2048
REGIONS = 4
TILES = 32
DEVICES = REGIONS * TILES
ROWS = 16
LANES = 128
BLOCKS = SOUNDINGS // LANES
CHUNKS = 4
LOGICAL = pl.DeviceIdType.LOGICAL
F32 = jnp.float32


def lane_iota(shape):
    return lax.broadcasted_iota(jnp.int32, shape, 1)


def row_iota(shape):
    return lax.broadcasted_iota(jnp.int32, shape, 0)


def total(values):
    return jnp.sum(values, keepdims=True)


def swap_pieces(parts):
    parts = list(parts)
    piece = lane_iota((8, LANES)) // 16
    for bit in (4, 2, 1):
        low = (piece & bit) == 0
        for first in range(8):
            if first & bit:
                continue
            a, b = parts[first], parts[first + bit]
            b_up = pltpu.roll(b, bit * 16, 1)
            a_down = pltpu.roll(a, LANES - bit * 16, 1)
            parts[first] = jnp.where(low, a, b_up)
            parts[first + bit] = jnp.where(low, a_down, b)
    return parts


def layers_of(group):
    return range(8 * group, min(8 * group + 8, LAYERS))


def fold_layers(terms):
    parts = []
    for term in terms:
        rows = [term[8 * n : 8 * n + 8] for n in range(GATES // 8)]
        while len(rows) > 1:
            rows = [sum(rows[n : n + 2][1:], rows[n]) for n in range(0, len(rows), 2)]
        parts.append(rows[0])
    parts += [jnp.zeros((8, LANES), F32)] * (8 - len(parts))
    row = row_iota((8, LANES))
    for bit in (1, 2, 4):
        low = (row & bit) == 0
        parts = [
            jnp.where(low, a, b) + pltpu.roll(jnp.where(low, b, a), bit, 0)
            for a, b in zip(parts[::2], parts[1::2])
        ]
    return parts[0]


def pick(source, group, index):
    low = index & (LANES - 1)
    high = index // LANES
    out = None
    for q in range(BLOCKS):
        block = source[group * 8 : group * 8 + 8, q * LANES : (q + 1) * LANES]
        taken = jnp.take_along_axis(block, low, axis=1, mode="promise_in_bounds")
        out = taken if out is None else jnp.where(high == q, taken, out)
    return out


def kernel(
    jac_in, misfit_in, model_in, vertical_in, lateral_in, order_in, order_flat, line_in,
    new_model, profile,
    misfit, model, vertical, lateral, order, order_s, line,
    jac, fields, vert, ordered, send_a, recv_a, grid, coef, c_grid, d_grid, edge, side,
    send_b, recv_b, back, resid, inverse, onehot, extended,
    sums_s, sums_r, part_s, part_r,
    in_sem, jac_sem, ring_s, ring_r, halo_s, halo_r, sums_ss, sums_rs,
):
    region = lax.axis_index("region")
    tile = lax.axis_index("tile")
    me = region * TILES + tile

    def place(device):
        return device

    def chunk_copy(chunk):
        columns = pl.ds(chunk * (SOUNDINGS // CHUNKS), SOUNDINGS // CHUNKS)
        return pltpu.make_async_copy(
            jac_in.at[:, :, columns], jac.at[:, :, columns], jac_sem.at[chunk]
        )

    loads = [
        pltpu.make_async_copy(src, dst, in_sem.at[n])
        for n, (src, dst) in enumerate(
            (
                (misfit_in, misfit),
                (vertical_in, vertical),
                (order_in, order),
                (order_flat, order_s),
                (lateral_in, lateral),
                (model_in, model),
                (line_in, line),
            )
        )
    ]
    vert[PADDED - 8 :, :] = jnp.zeros((8, SOUNDINGS), F32)
    chunk_copy(0).start()
    loads[0].start()
    loads[1].start()
    for chunk in range(1, CHUNKS):
        chunk_copy(chunk).start()
    for load in loads[2:]:
        load.start()

    barrier = pltpu.get_barrier_semaphore()

    def greet(i, carry):
        pl.semaphore_signal(
            barrier, inc=1, device_id=place((me + i) % DEVICES), device_id_type=LOGICAL
        )
        return carry

    lax.fori_loop(1, DEVICES, greet, 0)

    loads[0].wait()
    loads[1].wait()

    def local_part(block, sums):
        @pl.when(block % (BLOCKS // CHUNKS) == 0)
        def _():
            chunk_copy(block // (BLOCKS // CHUNKS)).wait()

        at = pl.ds(pl.multiple_of(block * LANES, LANES), LANES)

        gate_rows = misfit[:, at]
        for group in range(PADDED // 8):
            fields[8 * group : 8 * group + 8, at] = fold_layers(
                [jac[l, :, at].astype(F32) * gate_rows for l in layers_of(group)]
            )
        predicted = jnp.zeros((GATES, LANES), F32)
        for l in range(LAYERS):
            predicted = predicted + jac[l, :, at].astype(F32) * fields[l : l + 1, at]
        for group in range(PADDED // 8):
            fields[PADDED + 8 * group : PADDED + 8 * group + 8, at] = fold_layers(
                [jac[l, :, at].astype(F32) * predicted for l in layers_of(group)]
            )
        vert[0 : LAYERS - 1, at] = vertical[:, at]
        p = fields[0:PADDED, at]
        flux = vert[:, at] * (p - pltpu.roll(p, PADDED - 1, 0))
        applied = fields[PADDED:, at] + DAMPING * p + (flux - pltpu.roll(flux, 1, 0))
        fields[PADDED:, at] = applied
        return sums[0] + p * p, sums[1] + p * applied

    zero = jnp.zeros((PADDED, LANES), F32)
    square_sum, local_sum = lax.fori_loop(0, BLOCKS, local_part, (zero, zero))

    for load in loads[2:]:
        load.wait()
    pl.semaphore_wait(barrier, DEVICES - 1)

    def send_group(i, carry):
        first = (me // 32 + i) % 4 * 4

        def order_block(n, c):
            index = jnp.broadcast_to(order[pl.ds(first + n, 1), :], (8, LANES))
            for k in range(8):
                ordered[n, k] = pick(fields, k, index)
            return c

        lax.fori_loop(0, 4, order_block, 0, unroll=4)

        def turn_block(n, c):
            for j, message in enumerate(swap_pieces([ordered[n, k] for k in range(8)])):
                send_a[(first + n) * 8 + j] = message
            return c

        lax.fori_loop(0, 4, turn_block, 0, unroll=4)

        def post(n, c):
            peer = first * 8 + (me + n) % 32
            pltpu.make_async_remote_copy(
                src_ref=send_a.at[peer],
                dst_ref=recv_a.at[me],
                send_sem=ring_s.at[0],
                recv_sem=ring_r.at[0],
                device_id=place(peer),
                device_id_type=LOGICAL,
            ).start()
            return c

        lax.fori_loop(jnp.where(i == 0, 1, 0), 32, post, 0)
        return carry

    lax.fori_loop(0, 4, send_group, 0)
    recv_a[me] = send_a[me]

    places = row_iota((BLOCKS, LANES)) * LANES + lane_iota((BLOCKS, LANES))

    def invert(q, found):
        return jnp.where(places == order_s[q], q, found)

    inverse[...] = lax.fori_loop(
        0, SOUNDINGS, invert, jnp.zeros((BLOCKS, LANES), jnp.int32), unroll=16
    )

    run = row_iota((24, LANES))
    shift = jnp.where(run < 8, 0, jnp.where(run < 16, DEVICES - 1, DEVICES // 2))
    owner = (me + shift) & (DEVICES - 1)
    wanted = jnp.where((run & 7) < LINES_DEV, owner * LINES_DEV + (run & 7), -1)
    for block in range(BLOCKS):
        hit = line[block : block + 1, :] == wanted
        onehot[:, block * LANES : (block + 1) * LANES] = jnp.where(hit, 1.0, 0.0)
    extended[...] = jnp.ones_like(extended)
    extended[0:LAYERS, :] = model[...]

    def line_sums(slot, values):
        found = lax.dot_general(
            onehot[...], values, (((1,), (1,)), ((), ())),
            precision=lax.Precision.HIGHEST, preferred_element_type=F32,
        )
        for g in range(3):
            sums_s[g, slot, :, 0:PADDED] = found[8 * g : 8 * g + 8, :]

    sums_s[...] = jnp.zeros_like(sums_s)
    line_sums(0, extended[...])
    line_sums(1, fields[0:PADDED, :])

    def wait_ring(k, buffer, sem):
        whole = buffer.at[pl.ds(0, DEVICES - 1)]
        pltpu.make_async_copy(whole, whole, sem.at[k]).wait()

    wait_ring(0, recv_a, ring_r)
    wait_ring(0, send_a, ring_s)

    def place_row(i, carry):
        rows = swap_pieces([recv_a[i * 8 + j] for j in range(8)])
        for s in range(8):
            grid[i + 1, s * 8 : s * 8 + 8, :] = rows[s]
        grid[i + 1, LAYERS : LAYERS + 1, :] = lateral[pl.ds(i, 1), :]
        return carry

    lax.fori_loop(0, ROWS, place_row, 0, unroll=4)

    lane = lane_iota((PADDED, LANES))
    layer = row_iota((PADDED, LANES))

    def halo_copies(phase):
        ch = pl.ds(phase * PADDED, PADDED)
        above = (region + REGIONS - 1) % REGIONS * TILES + tile
        below = (region + 1) % REGIONS * TILES + tile
        left = region * TILES + (tile + TILES - 1) % TILES
        right = region * TILES + (tile + 1) % TILES
        pairs = (
            (grid.at[1, ch], grid.at[ROWS + 1, ch], above),
            (grid.at[ROWS, ch], grid.at[0, ch], below),
            (edge.at[phase, 0], side.at[phase, 1], left),
            (edge.at[phase, 1], side.at[phase, 0], right),
        )
        return [
            pltpu.make_async_remote_copy(
                src_ref=src, dst_ref=dst,
                send_sem=halo_s.at[phase, n], recv_sem=halo_r.at[phase, n],
                device_id=device, device_id_type=LOGICAL,
            )
            for n, (src, dst, device) in enumerate(pairs)
        ]

    def halo_start(phase):
        first = phase * PADDED
        west = jnp.zeros((PADDED, LANES), F32)
        east = jnp.zeros((PADDED, LANES), F32)
        for i in range(ROWS):
            row = grid[i + 1, first : first + PADDED, :]
            west = jnp.where(lane == i, row if i == 0 else pltpu.roll(row, i, 1), west)
            east = jnp.where(lane == i, pltpu.roll(row, i + 1, 1), east)
        edge[phase, 0] = west
        edge[phase, 1] = east
        copies = halo_copies(phase)
        for copy in copies:
            copy.start()
        return copies

    def halo_finish(phase, copies):
        for copy in copies:
            copy.wait()
        ch = slice(phase * PADDED, (phase + 1) * PADDED)

        @pl.when(region == 0)
        def _():
            grid[0, ch, :] = jnp.zeros((PADDED, LANES), F32)

        @pl.when(region == REGIONS - 1)
        def _():
            grid[ROWS + 1, ch, :] = jnp.zeros((PADDED, LANES), F32)

        @pl.when(tile == 0)
        def _():
            side[phase, 0] = jnp.zeros((PADDED, LANES), F32)

        @pl.when(tile == TILES - 1)
        def _():
            side[phase, 1] = jnp.zeros((PADDED, LANES), F32)

    def lateral_row(i, phase, west, east):
        ch = slice(phase * PADDED, (phase + 1) * PADDED)
        here = grid[i + 1, ch, :]
        up, down = grid[i, ch, :], grid[i + 2, ch, :]
        west_of = jnp.where(lane == 0, west, pltpu.roll(here, 1, 1))
        east_of = jnp.where(lane == LANES - 1, east, pltpu.roll(here, LANES - 1, 1))
        if phase == 0:
            own = here[LAYERS : LAYERS + 1]
            for n, (other, factor) in enumerate(
                ((up, 0.5), (down, 0.5), (west_of, 0.25), (east_of, 0.25))
            ):
                coef[i, n : n + 1, :] = factor * (own + other[LAYERS : LAYERS + 1])
        return (
            coef[i, 0:1, :] * (here - up)
            + coef[i, 1:2, :] * (here - down)
            + coef[i, 2:3, :] * (here - west_of)
            + coef[i, 3:4, :] * (here - east_of)
        )

    def lateral_part(phase, out):
        west, east = side[phase, 0], side[phase, 1]
        dots = [zero] * 2
        for i in range(ROWS):
            west_i = west if i == 0 else pltpu.roll(west, LANES - i, 1)
            value = lateral_row(i, phase, west_i, pltpu.roll(east, LANES - 1 - i, 1))
            out[i] = value
            if phase == 0:
                dots[i % 2] = dots[i % 2] + grid[i + 1, 0:PADDED, :] * value
        return dots[0] + dots[1]

    copies = halo_start(0)
    halo_finish(0, copies)
    lateral_sum = lateral_part(0, c_grid)

    inside = layer < LAYERS
    curve_part = total(jnp.where(inside, lateral_sum + local_sum, 0.0))
    square_part = total(square_sum)

    upper = row_iota((8, LANES)) < 4
    sublane = row_iota((8, LANES))

    def turn_pair(pair):
        parts = [None] * 8
        for k in range(4):
            a = c_grid[2 * pair, 8 * k : 8 * k + 8, :]
            b = c_grid[2 * pair + 1, 8 * k : 8 * k + 8, :]
            if k == 3:
                a = jnp.where(sublane == 6, curve_part, jnp.where(sublane == 7, square_part, a))
                b = jnp.where(sublane == 6, curve_part, jnp.where(sublane == 7, square_part, b))
            parts[k] = jnp.where(upper, a, pltpu.roll(b, 4, 0))
            parts[k + 4] = jnp.where(upper, pltpu.roll(a, 4, 0), b)
        for j, message in enumerate(swap_pieces(parts)):
            send_b[pair * 16 + j] = message[0:4]
            send_b[pair * 16 + 8 + j] = message[4:8]

    def send_half(i, carry):
        first = (me // 64 + i) % 2 * 4

        def turn(n, c):
            turn_pair(first + n)
            return c

        lax.fori_loop(0, 4, turn, 0, unroll=4)

        def post(n, c):
            peer = first * 16 + (me + n) % 64
            pltpu.make_async_remote_copy(
                src_ref=send_b.at[peer],
                dst_ref=recv_b.at[me],
                send_sem=ring_s.at[1],
                recv_sem=ring_r.at[1],
                device_id=place(peer),
                device_id_type=LOGICAL,
            ).start()
            return c

        lax.fori_loop(jnp.where(i == 0, 1, 0), 64, post, 0)
        return carry

    lax.fori_loop(0, 2, send_half, 0)
    recv_b[me] = send_b[me]

    def add_image(i, carry):
        grid[i + 1, PADDED:, :] = grid[i + 1, PADDED:, :] + c_grid[i]
        return carry

    lax.fori_loop(0, ROWS, add_image, 0, unroll=4)
    copies = halo_start(1)
    halo_finish(1, copies)
    lateral_part(1, d_grid)

    wait_ring(1, recv_b, ring_r)
    wait_ring(1, send_b, ring_s)

    def unpack_pair(pair, carried):
        words = [
            jnp.concatenate([recv_b[pair * 16 + j], recv_b[pair * 16 + 8 + j]], axis=0)
            for j in range(8)
        ]
        parts = swap_pieces(words)
        even = pl.ds(pl.multiple_of(pair * 2 * LANES, LANES), LANES)
        odd = pl.ds(pl.multiple_of(pair * 2 * LANES + LANES, LANES), LANES)
        for k in range(4):
            a = jnp.where(upper, parts[k], pltpu.roll(parts[k + 4], 4, 0))
            b = jnp.where(upper, pltpu.roll(parts[k], 4, 0), parts[k + 4])
            back[8 * k : 8 * k + 8, even] = a
            back[8 * k : 8 * k + 8, odd] = b
            if k == 3:
                carried = carried + a + b
        return carried

    carried = lax.fori_loop(0, BLOCKS // 2, unpack_pair, jnp.zeros((8, LANES), F32), unroll=4)
    curve = total(carried[6:7]) * (1.0 / 16)
    square = total(carried[7:8]) * (1.0 / 16)
    step_0 = square / curve

    def second_part(block, sums):
        at = pl.ds(pl.multiple_of(block * LANES, LANES), LANES)
        index = jnp.broadcast_to(inverse[pl.ds(block, 1), :], (8, LANES))
        taken = jnp.concatenate([pick(back, k, index) for k in range(4)], axis=0)
        applied = fields[PADDED:, at] + jnp.where(inside, taken, 0.0)
        r = fields[0:PADDED, at] - step_0 * applied
        resid[:, at] = r
        drop = r - pltpu.roll(r, PADDED - 1, 0)
        predicted = jnp.zeros((GATES, LANES), F32)
        for l in range(LAYERS):
            predicted = predicted + jac[l, :, at].astype(F32) * resid[l : l + 1, at]
        return (
            sums[0] + r * r,
            sums[1] + r * applied,
            sums[2] + vert[:, at] * (drop * drop) + DAMPING * (r * r),
            sums[3] + predicted * predicted,
        )

    r_square, r_image, r_curve, r_gates = lax.fori_loop(
        0, BLOCKS, second_part, (zero, zero, zero, jnp.zeros((GATES, LANES), F32))
    )

    def grid_curve(i, acc):
        r = grid[i + 1, 0:PADDED, :] - step_0 * grid[i + 1, PADDED:, :]
        return acc + r * (c_grid[i] - step_0 * d_grid[i])

    r_lateral = lax.fori_loop(0, ROWS, grid_curve, zero, unroll=4)
    r_curve = jnp.where(inside, r_curve + r_lateral, 0.0)

    def rows_sum(values):
        return jnp.sum(values, axis=0, keepdims=True)

    scalars = jnp.where(
        sublane == 0,
        rows_sum(r_square),
        jnp.where(
            sublane == 1,
            rows_sum(r_image),
            jnp.where(sublane == 2, rows_sum(r_curve) + rows_sum(r_gates), 0.0),
        ),
    )
    scalars = jnp.sum(scalars, axis=1, keepdims=True)
    part = rows_sum(jnp.where(sublane == lane_iota((8, LANES)), scalars, 0.0))
    part_s[0] = part
    part_r[me] = part

    def share(i, carry):
        pltpu.make_async_remote_copy(
            src_ref=part_s.at[0],
            dst_ref=part_r.at[me],
            send_sem=ring_s.at[2],
            recv_sem=ring_r.at[2],
            device_id=place((me + i) % DEVICES),
            device_id_type=LOGICAL,
        ).start()
        return carry

    lax.fori_loop(1, DEVICES, share, 0)

    line_sums(2, resid[...])
    sums_copies = []
    for g, offset in ((1, DEVICES - 1), (2, DEVICES // 2)):
        copy = pltpu.make_async_remote_copy(
            src_ref=sums_s.at[g],
            dst_ref=sums_r.at[g - 1],
            send_sem=sums_ss.at[g - 1],
            recv_sem=sums_rs.at[g - 1],
            device_id=place((me + offset) % DEVICES),
            device_id_type=LOGICAL,
        )
        copy.start()
        sums_copies.append(copy)

    wait_ring(2, part_r, ring_r)
    wait_ring(2, part_r, ring_s)
    for copy in sums_copies:
        copy.wait()

    sums = jnp.sum(part_r[...], axis=0)
    square_1, cross, curve_r = sums[:, 0:1], sums[:, 1:2], sums[:, 2:3]
    beta = square_1 / square
    curve_1 = curve_r + 2.0 * beta * cross + beta * beta * curve
    step_1 = square_1 / curve_1
    weight = step_0 + step_1 * beta
    new_model[...] = (
        model[...] + weight * fields[0:LAYERS, :] + step_1 * resid[0:LAYERS, :]
    )
    sums = [sums_s[0, n] + sums_r[0, n] + sums_r[1, n] for n in range(3)]
    count = sums[0][:, LAYERS : LAYERS + 1]
    means = (sums[0] + weight * sums[1] + step_1 * sums[2]) / count
    profile[...] = means[0:LINES_DEV, 0:LAYERS]


def body(jacobian, misfit, model, vertical_weight, lateral_weight, send_order, line_id):
    vmem = pl.BlockSpec(memory_space=pltpu.VMEM)
    dma = pltpu.SemaphoreType.DMA
    return pl.pallas_call(
        kernel,
        out_shape=(
            jax.ShapeDtypeStruct((LAYERS, SOUNDINGS), F32),
            jax.ShapeDtypeStruct((LINES_DEV, LAYERS), F32),
        ),
        in_specs=[pl.BlockSpec(memory_space=pltpu.HBM)] * 8,
        out_specs=(vmem, vmem),
        scratch_shapes=[
            pltpu.VMEM((GATES, SOUNDINGS), F32),
            pltpu.VMEM((LAYERS, SOUNDINGS), F32),
            pltpu.VMEM((LAYERS - 1, SOUNDINGS), F32),
            pltpu.VMEM((ROWS, LANES), F32),
            pltpu.VMEM((BLOCKS, LANES), jnp.int32),
            pltpu.SMEM((SOUNDINGS,), jnp.int32),
            pltpu.VMEM((BLOCKS, LANES), jnp.int32),
            pltpu.VMEM((LAYERS, GATES, SOUNDINGS), jnp.bfloat16),
            pltpu.VMEM((2 * PADDED, SOUNDINGS), F32),
            pltpu.VMEM((PADDED, SOUNDINGS), F32),
            pltpu.VMEM((4, 8, 8, LANES), F32),
            pltpu.VMEM((DEVICES, 8, LANES), F32),
            pltpu.VMEM((DEVICES, 8, LANES), F32),
            pltpu.VMEM((ROWS + 2, 2 * PADDED, LANES), F32),
            pltpu.VMEM((ROWS, 8, LANES), F32),
            pltpu.VMEM((ROWS, PADDED, LANES), F32),
            pltpu.VMEM((ROWS, PADDED, LANES), F32),
            pltpu.VMEM((2, 2, PADDED, LANES), F32),
            pltpu.VMEM((2, 2, PADDED, LANES), F32),
            pltpu.VMEM((DEVICES, 4, LANES), F32),
            pltpu.VMEM((DEVICES, 4, LANES), F32),
            pltpu.VMEM((PADDED, SOUNDINGS), F32),
            pltpu.VMEM((PADDED, SOUNDINGS), F32),
            pltpu.VMEM((BLOCKS, LANES), jnp.int32),
            pltpu.VMEM((24, SOUNDINGS), F32),
            pltpu.VMEM((PADDED, SOUNDINGS), F32),
            pltpu.VMEM((3, 3, 8, LANES), F32),
            pltpu.VMEM((2, 3, 8, LANES), F32),
            pltpu.VMEM((1, 1, LANES), F32),
            pltpu.VMEM((DEVICES, 1, LANES), F32),
            dma((7,)),
            dma((CHUNKS,)),
            dma((3,)),
            dma((3,)),
            dma((2, 4)),
            dma((2, 4)),
            dma((2,)),
            dma((2,)),
        ],
        compiler_params=pltpu.CompilerParams(
            collective_id=0, has_side_effects=True, vmem_limit_bytes=63 * 1024 * 1024
        ),
    )(
        jacobian.transpose(1, 0, 2),
        misfit,
        model,
        vertical_weight,
        lateral_weight,
        send_order.reshape(BLOCKS, LANES),
        send_order,
        line_id.reshape(BLOCKS, LANES),
    )


def solution(mesh):
    in_specs = (
        P(None, None, ("region", "tile")),
        P(None, ("region", "tile")),
        P(None, ("region", "tile")),
        P(None, ("region", "tile")),
        P("region", "tile"),
        P(("region", "tile")),
        P(("region", "tile")),
    )
    out_specs = (P(None, ("region", "tile")), P(("region", "tile"), None))
    return jax.shard_map(body, mesh=mesh, in_specs=in_specs, out_specs=out_specs, check_vma=False)
```

```python
import jax
import jax.numpy as jnp
from jax import lax
from jax.experimental import pallas as pl
from jax.experimental.pallas import tpu as pltpu
from jax.sharding import PartitionSpec as P

LINES_DEV = 4
DAMPING = 0.05
GATES = 40
LAYERS = 30
PADDED = 32
SOUNDINGS = 2048
REGIONS = 4
TILES = 32
DEVICES = REGIONS * TILES
ROWS = 16
LANES = 128
BLOCKS = SOUNDINGS // LANES
CHUNKS = 4
LOGICAL = pl.DeviceIdType.LOGICAL
F32 = jnp.float32


def lane_iota(shape):
    return lax.broadcasted_iota(jnp.int32, shape, 1)


def row_iota(shape):
    return lax.broadcasted_iota(jnp.int32, shape, 0)


def total(values):
    return jnp.sum(values, keepdims=True)


def swap_pieces(parts):
    parts = list(parts)
    piece = lane_iota((8, LANES)) // 16
    for bit in (4, 2, 1):
        low = (piece & bit) == 0
        for first in range(8):
            if first & bit:
                continue
            a, b = parts[first], parts[first + bit]
            b_up = pltpu.roll(b, bit * 16, 1)
            a_down = pltpu.roll(a, LANES - bit * 16, 1)
            parts[first] = jnp.where(low, a, b_up)
            parts[first + bit] = jnp.where(low, a_down, b)
    return parts


def layers_of(group):
    return range(8 * group, min(8 * group + 8, LAYERS))


def fold_layers(terms):
    parts = []
    for term in terms:
        rows = [term[8 * n : 8 * n + 8] for n in range(GATES // 8)]
        while len(rows) > 1:
            rows = [sum(rows[n : n + 2][1:], rows[n]) for n in range(0, len(rows), 2)]
        parts.append(rows[0])
    parts += [jnp.zeros((8, LANES), F32)] * (8 - len(parts))
    row = row_iota((8, LANES))
    for bit in (1, 2, 4):
        low = (row & bit) == 0
        parts = [
            jnp.where(low, a, b) + pltpu.roll(jnp.where(low, b, a), bit, 0)
            for a, b in zip(parts[::2], parts[1::2])
        ]
    return parts[0]


def pick(source, group, index):
    low = index & (LANES - 1)
    high = index // LANES
    out = None
    for q in range(BLOCKS):
        block = source[group * 8 : group * 8 + 8, q * LANES : (q + 1) * LANES]
        taken = jnp.take_along_axis(block, low, axis=1, mode="promise_in_bounds")
        out = taken if out is None else jnp.where(high == q, taken, out)
    return out


def kernel(
    jac_in, misfit_in, model_in, vertical_in, lateral_in, order_in, order_flat, line_in,
    new_model, profile,
    misfit, model, vertical, lateral, order, order_s, line,
    jac, fields, vert, ordered, send_p, recv_p, send_l, recv_l, grid, coef, c_grid, d_grid, edge, side,
    send_b, recv_b, back, resid, inverse, onehot, extended,
    sums_s, sums_r, part_s, part_r,
    in_sem, jac_sem, ring_s, ring_r, halo_s, halo_r, sums_ss, sums_rs,
):
    region = lax.axis_index("region")
    tile = lax.axis_index("tile")
    me = region * TILES + tile

    def place(device):
        return device

    def chunk_copy(chunk):
        columns = pl.ds(chunk * (SOUNDINGS // CHUNKS), SOUNDINGS // CHUNKS)
        return pltpu.make_async_copy(
            jac_in.at[:, :, columns], jac.at[:, :, columns], jac_sem.at[chunk]
        )

    loads = [
        pltpu.make_async_copy(src, dst, in_sem.at[n])
        for n, (src, dst) in enumerate(
            (
                (misfit_in, misfit),
                (vertical_in, vertical),
                (order_in, order),
                (order_flat, order_s),
                (lateral_in, lateral),
                (model_in, model),
                (line_in, line),
            )
        )
    ]
    vert[PADDED - 8 :, :] = jnp.zeros((8, SOUNDINGS), F32)
    chunk_copy(0).start()
    loads[0].start()
    loads[1].start()
    for chunk in range(1, CHUNKS):
        chunk_copy(chunk).start()
    for load in loads[2:]:
        load.start()

    barrier = pltpu.get_barrier_semaphore()

    def greet(i, carry):
        pl.semaphore_signal(
            barrier, inc=1, device_id=place((me + i) % DEVICES), device_id_type=LOGICAL
        )
        return carry

    lax.fori_loop(1, DEVICES, greet, 0)

    loads[0].wait()
    loads[1].wait()

    def local_part(block, sums):
        @pl.when(block % (BLOCKS // CHUNKS) == 0)
        def _():
            chunk_copy(block // (BLOCKS // CHUNKS)).wait()

        at = pl.ds(pl.multiple_of(block * LANES, LANES), LANES)

        gate_rows = misfit[:, at]
        for group in range(PADDED // 8):
            fields[8 * group : 8 * group + 8, at] = fold_layers(
                [jac[l, :, at].astype(F32) * gate_rows for l in layers_of(group)]
            )
        predicted = jnp.zeros((GATES, LANES), F32)
        for l in range(LAYERS):
            predicted = predicted + jac[l, :, at].astype(F32) * fields[l : l + 1, at]
        for group in range(PADDED // 8):
            fields[PADDED + 8 * group : PADDED + 8 * group + 8, at] = fold_layers(
                [jac[l, :, at].astype(F32) * predicted for l in layers_of(group)]
            )
        vert[0 : LAYERS - 1, at] = vertical[:, at]
        p = fields[0:PADDED, at]
        flux = vert[:, at] * (p - pltpu.roll(p, PADDED - 1, 0))
        applied = fields[PADDED:, at] + DAMPING * p + (flux - pltpu.roll(flux, 1, 0))
        fields[PADDED:, at] = applied
        return sums[0] + p * p, sums[1] + p * applied

    zero = jnp.zeros((PADDED, LANES), F32)
    square_sum, local_sum = lax.fori_loop(0, BLOCKS, local_part, (zero, zero))

    for load in loads[2:]:
        load.wait()

    upper = row_iota((8, LANES)) < 4
    sublane = row_iota((8, LANES))
    lane = lane_iota((PADDED, LANES))
    layer = row_iota((PADDED, LANES))
    inside = layer < LAYERS
    quarter_row = row_iota((4, LANES))
    quarter_lane = lane_iota((4, LANES))

    def pack_pair(pair, a, b, buffer):
        parts = [jnp.where(upper, a[k], pltpu.roll(b[k], 4, 0)) for k in range(4)]
        parts += [jnp.where(upper, pltpu.roll(a[k], 4, 0), b[k]) for k in range(4)]
        for j, message in enumerate(swap_pieces(parts)):
            buffer[pair * 16 + j] = message[0:4]
            buffer[pair * 16 + 8 + j] = message[4:8]

    def unpack_pair(pair, buffer):
        parts = swap_pieces(
            [
                jnp.concatenate([buffer[pair * 16 + j], buffer[pair * 16 + 8 + j]], axis=0)
                for j in range(8)
            ]
        )
        a = [jnp.where(upper, parts[k], pltpu.roll(parts[k + 4], 4, 0)) for k in range(4)]
        b = [jnp.where(upper, pltpu.roll(parts[k], 4, 0), parts[k + 4]) for k in range(4)]
        return a, b

    def post(ring, source, target, peer):
        pltpu.make_async_remote_copy(
            src_ref=source.at[peer],
            dst_ref=target.at[me],
            send_sem=ring_s.at[ring],
            recv_sem=ring_r.at[ring],
            device_id=peer,
            device_id_type=LOGICAL,
        ).start()

    def wait_ring(ring, buffer, sem):
        whole = buffer.at[pl.ds(0, DEVICES - 1)]
        pltpu.make_async_copy(whole, whole, sem.at[ring]).wait()

    def edge_of(message, side_of):
        out = jnp.zeros((4, LANES), F32)
        for i in range(ROWS):
            moved = pltpu.roll(message(i), (i - 15 * side_of) % LANES, 1)
            out = jnp.where(quarter_lane % 16 == i, moved, out)
        return out

    def weight_edge(side_of):
        out = jnp.zeros((4, LANES), F32)
        for i in range(ROWS):
            moved = jnp.broadcast_to(lateral[i : i + 1, :], (4, LANES))
            moved = pltpu.roll(moved, (112 + i + side_of) % LANES, 1)
            out = jnp.where((quarter_lane == 112 + i) & (quarter_row == 2), moved, out)
        return out

    edge[0, 0] = weight_edge(0)
    edge[0, 1] = weight_edge(1)

    pl.semaphore_wait(barrier, DEVICES - 1)

    places = row_iota((BLOCKS, LANES)) * LANES + lane_iota((BLOCKS, LANES))

    def invert(first, found):
        for q in range(16):
            found = jnp.where(places == order_s[first * 16 + q], first * 16 + q, found)
        return found

    def arrange(first, offset, buffer):
        def order_block(n, c):
            index = jnp.broadcast_to(order[pl.ds(first + n, 1), :], (8, LANES))
            for k in range(4):
                ordered[n, k] = pick(fields, offset + k, index)
            return c

        lax.fori_loop(0, 4, order_block, 0, unroll=4)
        for t in range(2):
            pack_pair(
                first // 2 + t,
                [ordered[2 * t, k] for k in range(4)],
                [ordered[2 * t + 1, k] for k in range(4)],
                buffer,
            )

    def send_group(i, found):
        first = (me // 32 + i) % 4 * 4
        arrange(first, 0, send_p)

        def step(n, found):
            post(0, send_p, recv_p, first * 8 + (me + n) % 32)
            return invert(i * 32 + n, found)

        return lax.fori_loop(jnp.where(i == 0, 1, 0), 32, step, found)

    inverse[...] = lax.fori_loop(
        0, 4, send_group, invert(0, jnp.zeros((BLOCKS, LANES), jnp.int32))
    )
    recv_p[me] = send_p[me]

    def arrange_local(i, c):
        arrange(i * 4, 4, send_l)
        return c

    lax.fori_loop(0, 4, arrange_local, 0)
    recv_l[me] = send_l[me]

    wait_ring(0, recv_p, ring_r)

    def place_pair(pair, c):
        a, b = unpack_pair(pair, recv_p)
        for h, rows in ((0, a), (1, b)):
            i = 2 * pair + h
            for k in range(4):
                grid[i + 1, 8 * k : 8 * k + 8, :] = rows[k]
            grid[i + 1, LAYERS : LAYERS + 1, :] = lateral[pl.ds(i, 1), :]
        return c

    def halo_start(phase):
        ch = pl.ds(phase * PADDED, PADDED)
        above = (region + REGIONS - 1) % REGIONS * TILES + tile
        below = (region + 1) % REGIONS * TILES + tile
        left = region * TILES + (tile + TILES - 1) % TILES
        right = region * TILES + (tile + 1) % TILES
        pairs = (
            (grid.at[1, ch], grid.at[ROWS + 1, ch], above),
            (grid.at[ROWS, ch], grid.at[0, ch], below),
            (edge.at[phase, 0], side.at[phase, 1], left),
            (edge.at[phase, 1], side.at[phase, 0], right),
        )
        copies = [
            pltpu.make_async_remote_copy(
                src_ref=src, dst_ref=dst,
                send_sem=halo_s.at[phase, n], recv_sem=halo_r.at[phase, n],
                device_id=device, device_id_type=LOGICAL,
            )
            for n, (src, dst, device) in enumerate(pairs)
        ]
        for copy in copies:
            copy.start()
        return copies

    def halo_finish(phase, copies):
        for copy in copies:
            copy.wait()
        ch = slice(phase * PADDED, (phase + 1) * PADDED)

        @pl.when(region == 0)
        def _():
            grid[0, ch, :] = jnp.zeros((PADDED, LANES), F32)

        @pl.when(region == REGIONS - 1)
        def _():
            grid[ROWS + 1, ch, :] = jnp.zeros((PADDED, LANES), F32)

        @pl.when(tile == 0)
        def _():
            side[phase, 0] = jnp.zeros((4, LANES), F32)

        @pl.when(tile == TILES - 1)
        def _():
            side[phase, 1] = jnp.zeros((4, LANES), F32)

    def lateral_row(i, phase, west, east):
        ch = slice(phase * PADDED, (phase + 1) * PADDED)
        here = grid[i + 1, ch, :]
        up, down = grid[i, ch, :], grid[i + 2, ch, :]
        west_of = jnp.where(lane == 0, west, pltpu.roll(here, 1, 1))
        east_of = jnp.where(lane == LANES - 1, east, pltpu.roll(here, LANES - 1, 1))
        if phase == 0:
            own = here[LAYERS : LAYERS + 1]
            for n, (other, factor) in enumerate(
                ((up, 0.5), (down, 0.5), (west_of, 0.25), (east_of, 0.25))
            ):
                coef[i, n : n + 1, :] = factor * (own + other[LAYERS : LAYERS + 1])
        return (
            coef[i, 0:1, :] * (here - up)
            + coef[i, 1:2, :] * (here - down)
            + coef[i, 2:3, :] * (here - west_of)
            + coef[i, 3:4, :] * (here - east_of)
        )

    def side_columns(phase, n, lane_to):
        twice = jnp.concatenate([side[phase, n], side[phase, n]], axis=0)
        both = jnp.where(upper, twice, pltpu.roll(twice, 64, 1))

        def column(i):
            return jnp.concatenate(
                [pltpu.roll(both, (lane_to - (s * 16 + i)) % LANES, 1) for s in range(4)], axis=0
            )

        return column

    def lateral_part(phase, out):
        west, east = side_columns(phase, 0, 0), side_columns(phase, 1, LANES - 1)
        dots = [zero] * 2
        for i in range(ROWS):
            value = lateral_row(i, phase, west(i), east(i))
            out[i] = value
            if phase == 0:
                dots[i % 2] = dots[i % 2] + grid[i + 1, 0:PADDED, :] * value
        return dots[0] + dots[1]

    place_pair(0, 0)
    place_pair(ROWS // 2 - 1, 0)
    for n in range(2):
        edge[0, n] = edge[0, n] + edge_of(lambda i: recv_p[i * 8 + 7 * n], n)
    copies = halo_start(0)

    def post_local(n, c):
        post(3, send_l, recv_l, (me + n) % DEVICES)
        return c

    lax.fori_loop(1, DEVICES, post_local, 0)
    lax.fori_loop(1, ROWS // 2 - 1, place_pair, 0, unroll=3)

    halo_finish(0, copies)
    lateral_sum = lateral_part(0, c_grid)

    curve_part = total(jnp.where(inside, lateral_sum + local_sum, 0.0))
    square_part = total(square_sum)

    def turn_pair(pair):
        rows = []
        for h in range(2):
            row = [c_grid[2 * pair + h, 8 * k : 8 * k + 8, :] for k in range(4)]
            row[3] = jnp.where(
                sublane == 6, curve_part, jnp.where(sublane == 7, square_part, row[3])
            )
            rows.append(row)
        pack_pair(pair, rows[0], rows[1], send_b)

    def send_half(i, carry):
        first = (me // 64 + i) % 2 * 4

        def turn(n, c):
            turn_pair(first + n)
            return c

        lax.fori_loop(0, 4, turn, 0, unroll=4)

        def step(n, c):
            post(1, send_b, recv_b, first * 16 + (me + n) % 64)
            return c

        lax.fori_loop(jnp.where(i == 0, 1, 0), 64, step, 0)
        return carry

    lax.fori_loop(0, 2, send_half, 0)
    recv_b[me] = send_b[me]

    wait_ring(3, recv_l, ring_r)

    def add_image(pair, c):
        a, b = unpack_pair(pair, recv_l)
        for h, rows in ((0, a), (1, b)):
            i = 2 * pair + h
            for k in range(4):
                ch = slice(8 * k, 8 * k + 8)
                grid[i + 1, PADDED + 8 * k : PADDED + 8 * k + 8, :] = rows[k] + c_grid[i, ch, :]
        return c

    lax.fori_loop(0, ROWS // 2, add_image, 0, unroll=4)
    for n in range(2):
        edge[1, n] = edge_of(lambda i: recv_l[i * 8 + 7 * n] + send_b[i * 8 + 7 * n], n)
    copies = halo_start(1)

    run = row_iota((24, LANES))
    shift = jnp.where(run < 8, 0, jnp.where(run < 16, DEVICES - 1, DEVICES // 2))
    owner = (me + shift) & (DEVICES - 1)
    wanted = jnp.where((run & 7) < LINES_DEV, owner * LINES_DEV + (run & 7), -1)
    for block in range(BLOCKS):
        hit = line[block : block + 1, :] == wanted
        onehot[:, block * LANES : (block + 1) * LANES] = jnp.where(hit, 1.0, 0.0)
    extended[...] = jnp.ones_like(extended)
    extended[0:LAYERS, :] = model[...]

    def line_sums(slot, values):
        found = lax.dot_general(
            onehot[...], values, (((1,), (1,)), ((), ())),
            precision=lax.Precision.HIGHEST, preferred_element_type=F32,
        )
        for g in range(3):
            sums_s[g, slot, :, 0:PADDED] = found[8 * g : 8 * g + 8, :]

    sums_s[...] = jnp.zeros_like(sums_s)
    line_sums(0, extended[...])
    line_sums(1, fields[0:PADDED, :])

    halo_finish(1, copies)
    lateral_part(1, d_grid)

    wait_ring(1, recv_b, ring_r)
    wait_ring(0, send_p, ring_s)
    wait_ring(3, send_l, ring_s)
    wait_ring(1, send_b, ring_s)

    def take_pair(pair, carried):
        a, b = unpack_pair(pair, recv_b)
        even = pl.ds(pl.multiple_of(pair * 2 * LANES, LANES), LANES)
        odd = pl.ds(pl.multiple_of(pair * 2 * LANES + LANES, LANES), LANES)
        for k in range(4):
            back[8 * k : 8 * k + 8, even] = a[k]
            back[8 * k : 8 * k + 8, odd] = b[k]
        return carried + a[3] + b[3]

    carried = lax.fori_loop(0, BLOCKS // 2, take_pair, jnp.zeros((8, LANES), F32), unroll=4)
    curve = total(carried[6:7]) * (1.0 / 16)
    square = total(carried[7:8]) * (1.0 / 16)
    step_0 = square / curve

    def second_part(block, sums):
        at = pl.ds(pl.multiple_of(block * LANES, LANES), LANES)
        index = jnp.broadcast_to(inverse[pl.ds(block, 1), :], (8, LANES))
        taken = jnp.concatenate([pick(back, k, index) for k in range(4)], axis=0)
        applied = fields[PADDED:, at] + jnp.where(inside, taken, 0.0)
        r = fields[0:PADDED, at] - step_0 * applied
        resid[:, at] = r
        drop = r - pltpu.roll(r, PADDED - 1, 0)
        predicted = jnp.zeros((GATES, LANES), F32)
        for l in range(LAYERS):
            predicted = predicted + jac[l, :, at].astype(F32) * resid[l : l + 1, at]
        return (
            sums[0] + r * r,
            sums[1] + r * applied,
            sums[2] + vert[:, at] * (drop * drop) + DAMPING * (r * r),
            sums[3] + predicted * predicted,
        )

    r_square, r_image, r_curve, r_gates = lax.fori_loop(
        0, BLOCKS, second_part, (zero, zero, zero, jnp.zeros((GATES, LANES), F32)), unroll=2
    )

    def grid_curve(i, acc):
        r = grid[i + 1, 0:PADDED, :] - step_0 * grid[i + 1, PADDED:, :]
        return acc + r * (c_grid[i] - step_0 * d_grid[i])

    r_lateral = lax.fori_loop(0, ROWS, grid_curve, zero, unroll=4)
    r_curve = jnp.where(inside, r_curve + r_lateral, 0.0)

    def rows_sum(values):
        return jnp.sum(values, axis=0, keepdims=True)

    scalars = jnp.where(
        sublane == 0,
        rows_sum(r_square),
        jnp.where(
            sublane == 1,
            rows_sum(r_image),
            jnp.where(sublane == 2, rows_sum(r_curve) + rows_sum(r_gates), 0.0),
        ),
    )
    scalars = jnp.sum(scalars, axis=1, keepdims=True)
    part = rows_sum(jnp.where(sublane == lane_iota((8, LANES)), scalars, 0.0))
    part_s[0] = part
    part_r[me] = part

    def share(i, carry):
        pltpu.make_async_remote_copy(
            src_ref=part_s.at[0],
            dst_ref=part_r.at[me],
            send_sem=ring_s.at[2],
            recv_sem=ring_r.at[2],
            device_id=place((me + i) % DEVICES),
            device_id_type=LOGICAL,
        ).start()
        return carry

    lax.fori_loop(1, DEVICES, share, 0)

    line_sums(2, resid[...])
    sums_copies = []
    for g, offset in ((1, DEVICES - 1), (2, DEVICES // 2)):
        copy = pltpu.make_async_remote_copy(
            src_ref=sums_s.at[g],
            dst_ref=sums_r.at[g - 1],
            send_sem=sums_ss.at[g - 1],
            recv_sem=sums_rs.at[g - 1],
            device_id=place((me + offset) % DEVICES),
            device_id_type=LOGICAL,
        )
        copy.start()
        sums_copies.append(copy)

    wait_ring(2, part_r, ring_r)
    wait_ring(2, part_r, ring_s)
    for copy in sums_copies:
        copy.wait()

    sums = jnp.sum(part_r[...], axis=0)
    square_1, cross, curve_r = sums[:, 0:1], sums[:, 1:2], sums[:, 2:3]
    beta = square_1 / square
    curve_1 = curve_r + 2.0 * beta * cross + beta * beta * curve
    step_1 = square_1 / curve_1
    weight = step_0 + step_1 * beta
    new_model[...] = (
        model[...] + weight * fields[0:LAYERS, :] + step_1 * resid[0:LAYERS, :]
    )
    sums = [sums_s[0, n] + sums_r[0, n] + sums_r[1, n] for n in range(3)]
    count = sums[0][:, LAYERS : LAYERS + 1]
    means = (sums[0] + weight * sums[1] + step_1 * sums[2]) / count
    profile[...] = means[0:LINES_DEV, 0:LAYERS]


def hand_on(model_in, profile_in, model_out, profile_out):
    model_out[...] = model_in[...]
    profile_out[...] = profile_in[...]


def body(jacobian, misfit, model, vertical_weight, lateral_weight, send_order, line_id):
    vmem = pl.BlockSpec(memory_space=pltpu.VMEM)
    dma = pltpu.SemaphoreType.DMA
    outs = pl.pallas_call(
        kernel,
        out_shape=(
            jax.ShapeDtypeStruct((LAYERS, SOUNDINGS), F32),
            jax.ShapeDtypeStruct((LINES_DEV, LAYERS), F32),
        ),
        in_specs=[pl.BlockSpec(memory_space=pltpu.HBM)] * 8,
        out_specs=(vmem, vmem),
        scratch_shapes=[
            pltpu.VMEM((GATES, SOUNDINGS), F32),
            pltpu.VMEM((LAYERS, SOUNDINGS), F32),
            pltpu.VMEM((LAYERS - 1, SOUNDINGS), F32),
            pltpu.VMEM((ROWS, LANES), F32),
            pltpu.VMEM((BLOCKS, LANES), jnp.int32),
            pltpu.SMEM((SOUNDINGS,), jnp.int32),
            pltpu.VMEM((BLOCKS, LANES), jnp.int32),
            pltpu.VMEM((LAYERS, GATES, SOUNDINGS), jnp.bfloat16),
            pltpu.VMEM((2 * PADDED, SOUNDINGS), F32),
            pltpu.VMEM((PADDED, SOUNDINGS), F32),
            pltpu.VMEM((4, 4, 8, LANES), F32),
            pltpu.VMEM((DEVICES, 4, LANES), F32),
            pltpu.VMEM((DEVICES, 4, LANES), F32),
            pltpu.VMEM((DEVICES, 4, LANES), F32),
            pltpu.VMEM((DEVICES, 4, LANES), F32),
            pltpu.VMEM((ROWS + 2, 2 * PADDED, LANES), F32),
            pltpu.VMEM((ROWS, 8, LANES), F32),
            pltpu.VMEM((ROWS, PADDED, LANES), F32),
            pltpu.VMEM((ROWS, PADDED, LANES), F32),
            pltpu.VMEM((2, 2, 4, LANES), F32),
            pltpu.VMEM((2, 2, 4, LANES), F32),
            pltpu.VMEM((DEVICES, 4, LANES), F32),
            pltpu.VMEM((DEVICES, 4, LANES), F32),
            pltpu.VMEM((PADDED, SOUNDINGS), F32),
            pltpu.VMEM((PADDED, SOUNDINGS), F32),
            pltpu.VMEM((BLOCKS, LANES), jnp.int32),
            pltpu.VMEM((24, SOUNDINGS), F32),
            pltpu.VMEM((PADDED, SOUNDINGS), F32),
            pltpu.VMEM((3, 3, 8, LANES), F32),
            pltpu.VMEM((2, 3, 8, LANES), F32),
            pltpu.VMEM((1, 1, LANES), F32),
            pltpu.VMEM((DEVICES, 1, LANES), F32),
            dma((7,)),
            dma((CHUNKS,)),
            dma((4,)),
            dma((4,)),
            dma((2, 4)),
            dma((2, 4)),
            dma((2,)),
            dma((2,)),
        ],
        compiler_params=pltpu.CompilerParams(
            collective_id=0, has_side_effects=True, vmem_limit_bytes=63 * 1024 * 1024
        ),
    )(
        jacobian.transpose(1, 0, 2),
        misfit,
        model,
        vertical_weight,
        lateral_weight,
        send_order.reshape(BLOCKS, LANES),
        send_order,
        line_id.reshape(BLOCKS, LANES),
    )
    return pl.pallas_call(
        hand_on,
        out_shape=(
            jax.ShapeDtypeStruct((LAYERS, SOUNDINGS), F32),
            jax.ShapeDtypeStruct((LINES_DEV, LAYERS), F32),
        ),
        in_specs=[vmem, vmem],
        out_specs=(vmem, vmem),
    )(*outs)


def solution(mesh):
    in_specs = (
        P(None, None, ("region", "tile")),
        P(None, ("region", "tile")),
        P(None, ("region", "tile")),
        P(None, ("region", "tile")),
        P("region", "tile"),
        P(("region", "tile")),
        P(("region", "tile")),
    )
    out_specs = (P(None, ("region", "tile")), P(("region", "tile"), None))
    return jax.shard_map(body, mesh=mesh, in_specs=in_specs, out_specs=out_specs, check_vma=False)
```

```python
import jax
import jax.numpy as jnp
from jax import lax
from jax.experimental import pallas as pl
from jax.experimental.pallas import tpu as pltpu
from jax.sharding import PartitionSpec as P

LINES_DEV = 4
DAMPING = 0.05
GATES = 40
LAYERS = 30
PADDED = 32
SOUNDINGS = 2048
REGIONS = 4
TILES = 32
DEVICES = REGIONS * TILES
ROWS = 16
LANES = 128
BLOCKS = SOUNDINGS // LANES
CHUNKS = 4
LOGICAL = pl.DeviceIdType.LOGICAL
F32 = jnp.float32


def lane_iota(shape):
    return lax.broadcasted_iota(jnp.int32, shape, 1)


def row_iota(shape):
    return lax.broadcasted_iota(jnp.int32, shape, 0)


def total(values):
    return jnp.sum(values, keepdims=True)


def swap_pieces(parts):
    parts = list(parts)
    piece = lane_iota((8, LANES)) // 16
    for bit in (4, 2, 1):
        low = (piece & bit) == 0
        for first in range(8):
            if first & bit:
                continue
            a, b = parts[first], parts[first + bit]
            b_up = pltpu.roll(b, bit * 16, 1)
            a_down = pltpu.roll(a, LANES - bit * 16, 1)
            parts[first] = jnp.where(low, a, b_up)
            parts[first + bit] = jnp.where(low, a_down, b)
    return parts


def layers_of(group):
    return range(8 * group, min(8 * group + 8, LAYERS))


def fold_layers(terms):
    parts = []
    for term in terms:
        rows = [term[8 * n : 8 * n + 8] for n in range(GATES // 8)]
        while len(rows) > 1:
            rows = [sum(rows[n : n + 2][1:], rows[n]) for n in range(0, len(rows), 2)]
        parts.append(rows[0])
    parts += [jnp.zeros((8, LANES), F32)] * (8 - len(parts))
    row = row_iota((8, LANES))
    for bit in (1, 2, 4):
        low = (row & bit) == 0
        parts = [
            jnp.where(low, a, b) + pltpu.roll(jnp.where(low, b, a), bit, 0)
            for a, b in zip(parts[::2], parts[1::2])
        ]
    return parts[0]


def pick(source, group, index):
    low = index & (LANES - 1)
    high = index // LANES
    out = None
    for q in range(BLOCKS):
        block = source[group * 8 : group * 8 + 8, q * LANES : (q + 1) * LANES]
        taken = jnp.take_along_axis(block, low, axis=1, mode="promise_in_bounds")
        out = taken if out is None else jnp.where(high == q, taken, out)
    return out


def kernel(
    jac_in, misfit_in, model_in, vertical_in, lateral_in, order_in, order_flat, line_in,
    new_model, profile,
    misfit, model, vertical, lateral, order, order_s, line,
    jac, fields, vert, ordered, send_p, recv_p, send_l, recv_l, grid, coef, c_grid, d_grid, edge, side,
    send_b, recv_b, back, resid, inverse, onehot, extended,
    sums_s, sums_r, part_s, part_r,
    in_sem, jac_sem, ring_s, ring_r, halo_s, halo_r, sums_ss, sums_rs,
):
    region = lax.axis_index("region")
    tile = lax.axis_index("tile")
    me = region * TILES + tile

    def place(device):
        return device

    def chunk_copy(chunk):
        columns = pl.ds(chunk * (SOUNDINGS // CHUNKS), SOUNDINGS // CHUNKS)
        return pltpu.make_async_copy(
            jac_in.at[:, :, columns], jac.at[:, :, columns], jac_sem.at[chunk]
        )

    loads = [
        pltpu.make_async_copy(src, dst, in_sem.at[n])
        for n, (src, dst) in enumerate(
            (
                (misfit_in, misfit),
                (vertical_in, vertical),
                (order_in, order),
                (order_flat, order_s),
                (lateral_in, lateral),
                (model_in, model),
                (line_in, line),
            )
        )
    ]
    vert[PADDED - 8 :, :] = jnp.zeros((8, SOUNDINGS), F32)
    chunk_copy(0).start()
    loads[0].start()
    loads[1].start()
    for chunk in range(1, CHUNKS):
        chunk_copy(chunk).start()
    for load in loads[2:]:
        load.start()

    barrier = pltpu.get_barrier_semaphore()

    def greet(i, carry):
        pl.semaphore_signal(
            barrier, inc=1, device_id=place((me + i) % DEVICES), device_id_type=LOGICAL
        )
        return carry

    lax.fori_loop(1, DEVICES, greet, 0)

    loads[0].wait()
    loads[1].wait()

    def local_part(block, sums):
        @pl.when(block % (BLOCKS // CHUNKS) == 0)
        def _():
            chunk_copy(block // (BLOCKS // CHUNKS)).wait()

        at = pl.ds(pl.multiple_of(block * LANES, LANES), LANES)

        gate_rows = misfit[:, at]
        for group in range(PADDED // 8):
            fields[8 * group : 8 * group + 8, at] = fold_layers(
                [jac[l, :, at].astype(F32) * gate_rows for l in layers_of(group)]
            )
        predicted = jnp.zeros((GATES, LANES), F32)
        for l in range(LAYERS):
            predicted = predicted + jac[l, :, at].astype(F32) * fields[l : l + 1, at]
        for group in range(PADDED // 8):
            fields[PADDED + 8 * group : PADDED + 8 * group + 8, at] = fold_layers(
                [jac[l, :, at].astype(F32) * predicted for l in layers_of(group)]
            )
        vert[0 : LAYERS - 1, at] = vertical[:, at]
        p = fields[0:PADDED, at]
        flux = vert[:, at] * (p - pltpu.roll(p, PADDED - 1, 0))
        applied = fields[PADDED:, at] + DAMPING * p + (flux - pltpu.roll(flux, 1, 0))
        fields[PADDED:, at] = applied
        return sums[0] + p * p, sums[1] + p * applied

    zero = jnp.zeros((PADDED, LANES), F32)
    square_sum, local_sum = lax.fori_loop(0, BLOCKS, local_part, (zero, zero))

    for load in loads[2:]:
        load.wait()

    upper = row_iota((8, LANES)) < 4
    sublane = row_iota((8, LANES))
    lane = lane_iota((PADDED, LANES))
    layer = row_iota((PADDED, LANES))
    inside = layer < LAYERS
    quarter_row = row_iota((4, LANES))
    quarter_lane = lane_iota((4, LANES))

    def pack_pair(pair, a, b, buffer):
        parts = [jnp.where(upper, a[k], pltpu.roll(b[k], 4, 0)) for k in range(4)]
        parts += [jnp.where(upper, pltpu.roll(a[k], 4, 0), b[k]) for k in range(4)]
        for j, message in enumerate(swap_pieces(parts)):
            buffer[pair * 16 + j] = message[0:4]
            buffer[pair * 16 + 8 + j] = message[4:8]

    def unpack_pair(pair, buffer):
        parts = swap_pieces(
            [
                jnp.concatenate([buffer[pair * 16 + j], buffer[pair * 16 + 8 + j]], axis=0)
                for j in range(8)
            ]
        )
        a = [jnp.where(upper, parts[k], pltpu.roll(parts[k + 4], 4, 0)) for k in range(4)]
        b = [jnp.where(upper, pltpu.roll(parts[k], 4, 0), parts[k + 4]) for k in range(4)]
        return a, b

    def post(ring, source, target, peer):
        pltpu.make_async_remote_copy(
            src_ref=source.at[peer],
            dst_ref=target.at[me],
            send_sem=ring_s.at[ring],
            recv_sem=ring_r.at[ring],
            device_id=peer,
            device_id_type=LOGICAL,
        ).start()

    def wait_ring(ring, buffer, sem):
        whole = buffer.at[pl.ds(0, DEVICES - 1)]
        pltpu.make_async_copy(whole, whole, sem.at[ring]).wait()

    def edge_of(message, side_of):
        out = jnp.zeros((4, LANES), F32)
        for i in range(ROWS):
            moved = pltpu.roll(message(i), (i - 15 * side_of) % LANES, 1)
            out = jnp.where(quarter_lane % 16 == i, moved, out)
        return out

    def weight_edge(side_of):
        out = jnp.zeros((4, LANES), F32)
        for i in range(ROWS):
            moved = jnp.broadcast_to(lateral[i : i + 1, :], (4, LANES))
            moved = pltpu.roll(moved, (112 + i + side_of) % LANES, 1)
            out = jnp.where((quarter_lane == 112 + i) & (quarter_row == 2), moved, out)
        return out

    edge[0, 0] = weight_edge(0)
    edge[0, 1] = weight_edge(1)

    places = row_iota((BLOCKS, LANES)) * LANES + lane_iota((BLOCKS, LANES))

    def invert(first, found):
        for q in range(16):
            found = jnp.where(places == order_s[first * 16 + q], first * 16 + q, found)
        return found

    def arrange(first, offset, buffer):
        def order_block(n, c):
            index = jnp.broadcast_to(order[pl.ds(first + n, 1), :], (8, LANES))
            for k in range(4):
                ordered[n, k] = pick(fields, offset + k, index)
            return c

        lax.fori_loop(0, 4, order_block, 0, unroll=4)
        for t in range(2):
            pack_pair(
                first // 2 + t,
                [ordered[2 * t, k] for k in range(4)],
                [ordered[2 * t + 1, k] for k in range(4)],
                buffer,
            )

    def arrange_direction(i, c):
        arrange(i * 4, 0, send_p)
        return c

    lax.fori_loop(0, 4, arrange_direction, 0)

    pl.semaphore_wait(barrier, DEVICES - 1)

    def post_direction(n, found):
        post(0, send_p, recv_p, (me + n) % DEVICES)
        return invert(n, found)

    inverse[...] = lax.fori_loop(
        1, DEVICES, post_direction, invert(0, jnp.zeros((BLOCKS, LANES), jnp.int32))
    )
    recv_p[me] = send_p[me]

    def arrange_local(i, c):
        arrange(i * 4, 4, send_l)
        return c

    lax.fori_loop(0, 4, arrange_local, 0)
    recv_l[me] = send_l[me]

    wait_ring(0, recv_p, ring_r)

    def place_pair(pair, c):
        a, b = unpack_pair(pair, recv_p)
        for h, rows in ((0, a), (1, b)):
            i = 2 * pair + h
            for k in range(4):
                grid[i + 1, 8 * k : 8 * k + 8, :] = rows[k]
            grid[i + 1, LAYERS : LAYERS + 1, :] = lateral[pl.ds(i, 1), :]
        return c

    def halo_start(phase):
        ch = pl.ds(phase * PADDED, PADDED)
        above = (region + REGIONS - 1) % REGIONS * TILES + tile
        below = (region + 1) % REGIONS * TILES + tile
        left = region * TILES + (tile + TILES - 1) % TILES
        right = region * TILES + (tile + 1) % TILES
        pairs = (
            (grid.at[1, ch], grid.at[ROWS + 1, ch], above),
            (grid.at[ROWS, ch], grid.at[0, ch], below),
            (edge.at[phase, 0], side.at[phase, 1], left),
            (edge.at[phase, 1], side.at[phase, 0], right),
        )
        copies = [
            pltpu.make_async_remote_copy(
                src_ref=src, dst_ref=dst,
                send_sem=halo_s.at[phase, n], recv_sem=halo_r.at[phase, n],
                device_id=device, device_id_type=LOGICAL,
            )
            for n, (src, dst, device) in enumerate(pairs)
        ]
        for copy in copies:
            copy.start()
        return copies

    def halo_finish(phase, copies):
        for copy in copies:
            copy.wait()
        ch = slice(phase * PADDED, (phase + 1) * PADDED)

        @pl.when(region == 0)
        def _():
            grid[0, ch, :] = jnp.zeros((PADDED, LANES), F32)

        @pl.when(region == REGIONS - 1)
        def _():
            grid[ROWS + 1, ch, :] = jnp.zeros((PADDED, LANES), F32)

        @pl.when(tile == 0)
        def _():
            side[phase, 0] = jnp.zeros((4, LANES), F32)

        @pl.when(tile == TILES - 1)
        def _():
            side[phase, 1] = jnp.zeros((4, LANES), F32)

    def lateral_row(i, phase, west, east):
        ch = slice(phase * PADDED, (phase + 1) * PADDED)
        here = grid[i + 1, ch, :]
        up, down = grid[i, ch, :], grid[i + 2, ch, :]
        west_of = jnp.where(lane == 0, west, pltpu.roll(here, 1, 1))
        east_of = jnp.where(lane == LANES - 1, east, pltpu.roll(here, LANES - 1, 1))
        if phase == 0:
            own = here[LAYERS : LAYERS + 1]
            for n, (other, factor) in enumerate(
                ((up, 0.5), (down, 0.5), (west_of, 0.25), (east_of, 0.25))
            ):
                coef[i, n : n + 1, :] = factor * (own + other[LAYERS : LAYERS + 1])
        return (
            coef[i, 0:1, :] * (here - up)
            + coef[i, 1:2, :] * (here - down)
            + coef[i, 2:3, :] * (here - west_of)
            + coef[i, 3:4, :] * (here - east_of)
        )

    def side_columns(phase, n, lane_to):
        twice = jnp.concatenate([side[phase, n], side[phase, n]], axis=0)
        both = jnp.where(upper, twice, pltpu.roll(twice, 64, 1))

        def column(i):
            return jnp.concatenate(
                [pltpu.roll(both, (lane_to - (s * 16 + i)) % LANES, 1) for s in range(4)], axis=0
            )

        return column

    def lateral_part(phase, out):
        west, east = side_columns(phase, 0, 0), side_columns(phase, 1, LANES - 1)
        dots = [zero] * 2
        for i in range(ROWS):
            value = lateral_row(i, phase, west(i), east(i))
            out[i] = value
            if phase == 0:
                dots[i % 2] = dots[i % 2] + grid[i + 1, 0:PADDED, :] * value
        return dots[0] + dots[1]

    place_pair(0, 0)
    place_pair(ROWS // 2 - 1, 0)
    for n in range(2):
        edge[0, n] = edge[0, n] + edge_of(lambda i: recv_p[i * 8 + 7 * n], n)
    copies = halo_start(0)

    def post_local(n, c):
        post(3, send_l, recv_l, (me + n) % DEVICES)
        return c

    lax.fori_loop(1, DEVICES, post_local, 0)
    lax.fori_loop(1, ROWS // 2 - 1, place_pair, 0, unroll=3)

    halo_finish(0, copies)
    lateral_sum = lateral_part(0, c_grid)

    curve_part = total(jnp.where(inside, lateral_sum + local_sum, 0.0))
    square_part = total(square_sum)

    def turn_pair(pair):
        rows = []
        for h in range(2):
            row = [c_grid[2 * pair + h, 8 * k : 8 * k + 8, :] for k in range(4)]
            row[3] = jnp.where(
                sublane == 6, curve_part, jnp.where(sublane == 7, square_part, row[3])
            )
            rows.append(row)
        pack_pair(pair, rows[0], rows[1], send_b)

    def send_half(i, carry):
        first = (me // 64 + i) % 2 * 4

        def turn(n, c):
            turn_pair(first + n)
            return c

        lax.fori_loop(0, 4, turn, 0, unroll=4)

        def step(n, c):
            post(1, send_b, recv_b, first * 16 + (me + n) % 64)
            return c

        lax.fori_loop(jnp.where(i == 0, 1, 0), 64, step, 0)
        return carry

    lax.fori_loop(0, 2, send_half, 0)
    recv_b[me] = send_b[me]

    wait_ring(3, recv_l, ring_r)

    def add_image(pair, c):
        a, b = unpack_pair(pair, recv_l)
        for h, rows in ((0, a), (1, b)):
            i = 2 * pair + h
            for k in range(4):
                ch = slice(8 * k, 8 * k + 8)
                grid[i + 1, PADDED + 8 * k : PADDED + 8 * k + 8, :] = rows[k] + c_grid[i, ch, :]
        return c

    lax.fori_loop(0, ROWS // 2, add_image, 0, unroll=4)
    for n in range(2):
        edge[1, n] = edge_of(lambda i: recv_l[i * 8 + 7 * n] + send_b[i * 8 + 7 * n], n)
    copies = halo_start(1)

    run = row_iota((24, LANES))
    shift = jnp.where(run < 8, 0, jnp.where(run < 16, DEVICES - 1, DEVICES // 2))
    owner = (me + shift) & (DEVICES - 1)
    wanted = jnp.where((run & 7) < LINES_DEV, owner * LINES_DEV + (run & 7), -1)
    for block in range(BLOCKS):
        hit = line[block : block + 1, :] == wanted
        onehot[:, block * LANES : (block + 1) * LANES] = jnp.where(hit, 1.0, 0.0)
    extended[...] = jnp.ones_like(extended)
    extended[0:LAYERS, :] = model[...]

    def line_sums(slot, values):
        found = lax.dot_general(
            onehot[...], values, (((1,), (1,)), ((), ())),
            precision=lax.Precision.HIGHEST, preferred_element_type=F32,
        )
        for g in range(3):
            sums_s[g, slot, :, 0:PADDED] = found[8 * g : 8 * g + 8, :]

    sums_s[...] = jnp.zeros_like(sums_s)
    line_sums(0, extended[...])
    line_sums(1, fields[0:PADDED, :])

    halo_finish(1, copies)
    lateral_part(1, d_grid)

    wait_ring(1, recv_b, ring_r)
    wait_ring(0, send_p, ring_s)
    wait_ring(3, send_l, ring_s)
    wait_ring(1, send_b, ring_s)

    def take_pair(pair, carried):
        a, b = unpack_pair(pair, recv_b)
        even = pl.ds(pl.multiple_of(pair * 2 * LANES, LANES), LANES)
        odd = pl.ds(pl.multiple_of(pair * 2 * LANES + LANES, LANES), LANES)
        for k in range(4):
            back[8 * k : 8 * k + 8, even] = a[k]
            back[8 * k : 8 * k + 8, odd] = b[k]
        return carried + a[3] + b[3]

    carried = lax.fori_loop(0, BLOCKS // 2, take_pair, jnp.zeros((8, LANES), F32), unroll=4)
    curve = total(carried[6:7]) * (1.0 / 16)
    square = total(carried[7:8]) * (1.0 / 16)
    step_0 = square / curve

    def second_part(block, sums):
        at = pl.ds(pl.multiple_of(block * LANES, LANES), LANES)
        index = jnp.broadcast_to(inverse[pl.ds(block, 1), :], (8, LANES))
        taken = jnp.concatenate([pick(back, k, index) for k in range(4)], axis=0)
        applied = fields[PADDED:, at] + jnp.where(inside, taken, 0.0)
        r = fields[0:PADDED, at] - step_0 * applied
        resid[:, at] = r
        drop = r - pltpu.roll(r, PADDED - 1, 0)
        predicted = jnp.zeros((GATES, LANES), F32)
        for l in range(LAYERS):
            predicted = predicted + jac[l, :, at].astype(F32) * resid[l : l + 1, at]
        return (
            sums[0] + r * r,
            sums[1] + r * applied,
            sums[2] + vert[:, at] * (drop * drop) + DAMPING * (r * r),
            sums[3] + predicted * predicted,
        )

    r_square, r_image, r_curve, r_gates = lax.fori_loop(
        0, BLOCKS, second_part, (zero, zero, zero, jnp.zeros((GATES, LANES), F32)), unroll=2
    )

    def grid_curve(i, acc):
        r = grid[i + 1, 0:PADDED, :] - step_0 * grid[i + 1, PADDED:, :]
        return acc + r * (c_grid[i] - step_0 * d_grid[i])

    r_lateral = lax.fori_loop(0, ROWS, grid_curve, zero, unroll=4)
    r_curve = jnp.where(inside, r_curve + r_lateral, 0.0)

    def rows_sum(values):
        return jnp.sum(values, axis=0, keepdims=True)

    scalars = jnp.where(
        sublane == 0,
        rows_sum(r_square),
        jnp.where(
            sublane == 1,
            rows_sum(r_image),
            jnp.where(sublane == 2, rows_sum(r_curve) + rows_sum(r_gates), 0.0),
        ),
    )
    scalars = jnp.sum(scalars, axis=1, keepdims=True)
    part = rows_sum(jnp.where(sublane == lane_iota((8, LANES)), scalars, 0.0))
    part_s[0] = part
    part_r[me] = part

    def share(i, carry):
        pltpu.make_async_remote_copy(
            src_ref=part_s.at[0],
            dst_ref=part_r.at[me],
            send_sem=ring_s.at[2],
            recv_sem=ring_r.at[2],
            device_id=place((me + i) % DEVICES),
            device_id_type=LOGICAL,
        ).start()
        return carry

    lax.fori_loop(1, DEVICES, share, 0)

    line_sums(2, resid[...])
    sums_copies = []
    for g, offset in ((1, DEVICES - 1), (2, DEVICES // 2)):
        copy = pltpu.make_async_remote_copy(
            src_ref=sums_s.at[g],
            dst_ref=sums_r.at[g - 1],
            send_sem=sums_ss.at[g - 1],
            recv_sem=sums_rs.at[g - 1],
            device_id=place((me + offset) % DEVICES),
            device_id_type=LOGICAL,
        )
        copy.start()
        sums_copies.append(copy)

    wait_ring(2, part_r, ring_r)
    wait_ring(2, part_r, ring_s)
    for copy in sums_copies:
        copy.wait()

    sums = jnp.sum(part_r[...], axis=0)
    square_1, cross, curve_r = sums[:, 0:1], sums[:, 1:2], sums[:, 2:3]
    beta = square_1 / square
    curve_1 = curve_r + 2.0 * beta * cross + beta * beta * curve
    step_1 = square_1 / curve_1
    weight = step_0 + step_1 * beta
    new_model[...] = (
        model[...] + weight * fields[0:LAYERS, :] + step_1 * resid[0:LAYERS, :]
    )
    sums = [sums_s[0, n] + sums_r[0, n] + sums_r[1, n] for n in range(3)]
    count = sums[0][:, LAYERS : LAYERS + 1]
    means = (sums[0] + weight * sums[1] + step_1 * sums[2]) / count
    profile[...] = means[0:LINES_DEV, 0:LAYERS]


def hand_on(model_in, profile_in, model_out, profile_out):
    model_out[...] = model_in[...]
    profile_out[...] = profile_in[...]


def body(jacobian, misfit, model, vertical_weight, lateral_weight, send_order, line_id):
    vmem = pl.BlockSpec(memory_space=pltpu.VMEM)
    dma = pltpu.SemaphoreType.DMA
    outs = pl.pallas_call(
        kernel,
        out_shape=(
            jax.ShapeDtypeStruct((LAYERS, SOUNDINGS), F32),
            jax.ShapeDtypeStruct((LINES_DEV, LAYERS), F32),
        ),
        in_specs=[pl.BlockSpec(memory_space=pltpu.HBM)] * 8,
        out_specs=(vmem, vmem),
        scratch_shapes=[
            pltpu.VMEM((GATES, SOUNDINGS), F32),
            pltpu.VMEM((LAYERS, SOUNDINGS), F32),
            pltpu.VMEM((LAYERS - 1, SOUNDINGS), F32),
            pltpu.VMEM((ROWS, LANES), F32),
            pltpu.VMEM((BLOCKS, LANES), jnp.int32),
            pltpu.SMEM((SOUNDINGS,), jnp.int32),
            pltpu.VMEM((BLOCKS, LANES), jnp.int32),
            pltpu.VMEM((LAYERS, GATES, SOUNDINGS), jnp.bfloat16),
            pltpu.VMEM((2 * PADDED, SOUNDINGS), F32),
            pltpu.VMEM((PADDED, SOUNDINGS), F32),
            pltpu.VMEM((4, 4, 8, LANES), F32),
            pltpu.VMEM((DEVICES, 4, LANES), F32),
            pltpu.VMEM((DEVICES, 4, LANES), F32),
            pltpu.VMEM((DEVICES, 4, LANES), F32),
            pltpu.VMEM((DEVICES, 4, LANES), F32),
            pltpu.VMEM((ROWS + 2, 2 * PADDED, LANES), F32),
            pltpu.VMEM((ROWS, 8, LANES), F32),
            pltpu.VMEM((ROWS, PADDED, LANES), F32),
            pltpu.VMEM((ROWS, PADDED, LANES), F32),
            pltpu.VMEM((2, 2, 4, LANES), F32),
            pltpu.VMEM((2, 2, 4, LANES), F32),
            pltpu.VMEM((DEVICES, 4, LANES), F32),
            pltpu.VMEM((DEVICES, 4, LANES), F32),
            pltpu.VMEM((PADDED, SOUNDINGS), F32),
            pltpu.VMEM((PADDED, SOUNDINGS), F32),
            pltpu.VMEM((BLOCKS, LANES), jnp.int32),
            pltpu.VMEM((24, SOUNDINGS), F32),
            pltpu.VMEM((PADDED, SOUNDINGS), F32),
            pltpu.VMEM((3, 3, 8, LANES), F32),
            pltpu.VMEM((2, 3, 8, LANES), F32),
            pltpu.VMEM((1, 1, LANES), F32),
            pltpu.VMEM((DEVICES, 1, LANES), F32),
            dma((7,)),
            dma((CHUNKS,)),
            dma((4,)),
            dma((4,)),
            dma((2, 4)),
            dma((2, 4)),
            dma((2,)),
            dma((2,)),
        ],
        compiler_params=pltpu.CompilerParams(
            collective_id=0, has_side_effects=True, vmem_limit_bytes=63 * 1024 * 1024
        ),
    )(
        jacobian.transpose(1, 0, 2),
        misfit,
        model,
        vertical_weight,
        lateral_weight,
        send_order.reshape(BLOCKS, LANES),
        send_order,
        line_id.reshape(BLOCKS, LANES),
    )
    return pl.pallas_call(
        hand_on,
        out_shape=(
            jax.ShapeDtypeStruct((LAYERS, SOUNDINGS), F32),
            jax.ShapeDtypeStruct((LINES_DEV, LAYERS), F32),
        ),
        in_specs=[vmem, vmem],
        out_specs=(vmem, vmem),
    )(*outs)


def solution(mesh):
    in_specs = (
        P(None, None, ("region", "tile")),
        P(None, ("region", "tile")),
        P(None, ("region", "tile")),
        P(None, ("region", "tile")),
        P("region", "tile"),
        P(("region", "tile")),
        P(("region", "tile")),
    )
    out_specs = (P(None, ("region", "tile")), P(("region", "tile"), None))
    return jax.shard_map(body, mesh=mesh, in_specs=in_specs, out_specs=out_specs, check_vma=False)
```

```python
import jax
import jax.numpy as jnp
from jax import lax
from jax.experimental import pallas as pl
from jax.experimental.pallas import tpu as pltpu
from jax.sharding import PartitionSpec as P

LINES_DEV = 4
DAMPING = 0.05
GATES = 40
LAYERS = 30
PADDED = 32
SOUNDINGS = 2048
REGIONS = 4
TILES = 32
DEVICES = REGIONS * TILES
ROWS = 16
LANES = 128
BLOCKS = SOUNDINGS // LANES
CHUNKS = 4
LOGICAL = pl.DeviceIdType.LOGICAL
F32 = jnp.float32


def lane_iota(shape):
    return lax.broadcasted_iota(jnp.int32, shape, 1)


def row_iota(shape):
    return lax.broadcasted_iota(jnp.int32, shape, 0)


def total(values):
    return jnp.sum(values, keepdims=True)


def swap_pieces(parts):
    parts = list(parts)
    piece = lane_iota((8, LANES)) // 16
    for bit in (4, 2, 1):
        low = (piece & bit) == 0
        for first in range(8):
            if first & bit:
                continue
            a, b = parts[first], parts[first + bit]
            b_up = pltpu.roll(b, bit * 16, 1)
            a_down = pltpu.roll(a, LANES - bit * 16, 1)
            parts[first] = jnp.where(low, a, b_up)
            parts[first + bit] = jnp.where(low, a_down, b)
    return parts


def layers_of(group):
    return range(8 * group, min(8 * group + 8, LAYERS))


def fold_layers(terms):
    parts = []
    for term in terms:
        rows = [term[8 * n : 8 * n + 8] for n in range(GATES // 8)]
        while len(rows) > 1:
            rows = [sum(rows[n : n + 2][1:], rows[n]) for n in range(0, len(rows), 2)]
        parts.append(rows[0])
    parts += [jnp.zeros((8, LANES), F32)] * (8 - len(parts))
    row = row_iota((8, LANES))
    for bit in (1, 2, 4):
        low = (row & bit) == 0
        parts = [
            jnp.where(low, a, b) + pltpu.roll(jnp.where(low, b, a), bit, 0)
            for a, b in zip(parts[::2], parts[1::2])
        ]
    return parts[0]


def pick(source, group, index):
    low = index & (LANES - 1)
    high = index // LANES
    out = None
    for q in range(BLOCKS):
        block = source[group * 8 : group * 8 + 8, q * LANES : (q + 1) * LANES]
        taken = jnp.take_along_axis(block, low, axis=1, mode="promise_in_bounds")
        out = taken if out is None else jnp.where(high == q, taken, out)
    return out


def kernel(
    jac_in, misfit_in, model_in, vertical_in, lateral_in, order_in, order_flat, line_in,
    new_model, profile,
    misfit, model, vertical, lateral, order, order_s, line,
    jac, fields, vert, ordered, send_p, recv_p, send_l, recv_l, grid, coef, c_grid, d_grid, edge, side,
    send_b, recv_b, back, resid, inverse, onehot, extended,
    sums_s, sums_r, part_s, part_r,
    in_sem, jac_sem, ring_s, ring_r, halo_s, halo_r, sums_ss, sums_rs,
):
    region = lax.axis_index("region")
    tile = lax.axis_index("tile")
    me = region * TILES + tile

    def place(device):
        return device

    def chunk_copy(chunk):
        columns = pl.ds(chunk * (SOUNDINGS // CHUNKS), SOUNDINGS // CHUNKS)
        return pltpu.make_async_copy(
            jac_in.at[:, :, columns], jac.at[:, :, columns], jac_sem.at[chunk]
        )

    loads = [
        pltpu.make_async_copy(src, dst, in_sem.at[n])
        for n, (src, dst) in enumerate(
            (
                (misfit_in, misfit),
                (vertical_in, vertical),
                (order_in, order),
                (order_flat, order_s),
                (lateral_in, lateral),
                (model_in, model),
                (line_in, line),
            )
        )
    ]
    vert[PADDED - 8 :, :] = jnp.zeros((8, SOUNDINGS), F32)
    chunk_copy(0).start()
    loads[0].start()
    loads[1].start()
    for chunk in range(1, CHUNKS):
        chunk_copy(chunk).start()
    for load in loads[2:]:
        load.start()

    barrier = pltpu.get_barrier_semaphore()

    def greet(i, carry):
        pl.semaphore_signal(
            barrier, inc=1, device_id=place((me + i) % DEVICES), device_id_type=LOGICAL
        )
        return carry

    lax.fori_loop(1, DEVICES, greet, 0)

    loads[0].wait()
    loads[1].wait()

    def local_part(block, sums):
        @pl.when(block % (BLOCKS // CHUNKS) == 0)
        def _():
            chunk_copy(block // (BLOCKS // CHUNKS)).wait()

        at = pl.ds(pl.multiple_of(block * LANES, LANES), LANES)

        gate_rows = misfit[:, at]
        for group in range(PADDED // 8):
            fields[8 * group : 8 * group + 8, at] = fold_layers(
                [jac[l, :, at].astype(F32) * gate_rows for l in layers_of(group)]
            )
        predicted = jnp.zeros((GATES, LANES), F32)
        for l in range(LAYERS):
            predicted = predicted + jac[l, :, at].astype(F32) * fields[l : l + 1, at]
        for group in range(PADDED // 8):
            fields[PADDED + 8 * group : PADDED + 8 * group + 8, at] = fold_layers(
                [jac[l, :, at].astype(F32) * predicted for l in layers_of(group)]
            )
        vert[0 : LAYERS - 1, at] = vertical[:, at]
        p = fields[0:PADDED, at]
        flux = vert[:, at] * (p - pltpu.roll(p, PADDED - 1, 0))
        applied = fields[PADDED:, at] + DAMPING * p + (flux - pltpu.roll(flux, 1, 0))
        fields[PADDED:, at] = applied
        return sums[0] + p * p, sums[1] + p * applied

    zero = jnp.zeros((PADDED, LANES), F32)
    square_sum, local_sum = lax.fori_loop(0, BLOCKS, local_part, (zero, zero))

    for load in loads[2:]:
        load.wait()

    upper = row_iota((8, LANES)) < 4
    sublane = row_iota((8, LANES))
    lane = lane_iota((PADDED, LANES))
    layer = row_iota((PADDED, LANES))
    inside = layer < LAYERS
    quarter_row = row_iota((4, LANES))
    quarter_lane = lane_iota((4, LANES))

    def pack_pair(pair, a, b, buffer):
        parts = [jnp.where(upper, a[k], pltpu.roll(b[k], 4, 0)) for k in range(4)]
        parts += [jnp.where(upper, pltpu.roll(a[k], 4, 0), b[k]) for k in range(4)]
        for j, message in enumerate(swap_pieces(parts)):
            buffer[pair * 16 + j] = message[0:4]
            buffer[pair * 16 + 8 + j] = message[4:8]

    def unpack_pair(pair, buffer):
        parts = swap_pieces(
            [
                jnp.concatenate([buffer[pair * 16 + j], buffer[pair * 16 + 8 + j]], axis=0)
                for j in range(8)
            ]
        )
        a = [jnp.where(upper, parts[k], pltpu.roll(parts[k + 4], 4, 0)) for k in range(4)]
        b = [jnp.where(upper, pltpu.roll(parts[k], 4, 0), parts[k + 4]) for k in range(4)]
        return a, b

    def post(ring, source, target, peer):
        pltpu.make_async_remote_copy(
            src_ref=source.at[peer],
            dst_ref=target.at[me],
            send_sem=ring_s.at[ring],
            recv_sem=ring_r.at[ring],
            device_id=peer,
            device_id_type=LOGICAL,
        ).start()

    def wait_ring(ring, buffer, sem):
        whole = buffer.at[pl.ds(0, DEVICES - 1)]
        pltpu.make_async_copy(whole, whole, sem.at[ring]).wait()

    def edge_of(message, side_of):
        out = jnp.zeros((4, LANES), F32)
        for i in range(ROWS):
            moved = pltpu.roll(message(i), (i - 15 * side_of) % LANES, 1)
            out = jnp.where(quarter_lane % 16 == i, moved, out)
        return out

    def weight_edge(side_of):
        out = jnp.zeros((4, LANES), F32)
        for i in range(ROWS):
            moved = jnp.broadcast_to(lateral[i : i + 1, :], (4, LANES))
            moved = pltpu.roll(moved, (112 + i + side_of) % LANES, 1)
            out = jnp.where((quarter_lane == 112 + i) & (quarter_row == 2), moved, out)
        return out

    edge[0, 0] = weight_edge(0)
    edge[0, 1] = weight_edge(1)

    places = row_iota((BLOCKS, LANES)) * LANES + lane_iota((BLOCKS, LANES))

    def invert(first, found):
        for q in range(16):
            found = jnp.where(places == order_s[first * 16 + q], first * 16 + q, found)
        return found

    def arrange(first, offset, buffer):
        def order_block(n, c):
            index = jnp.broadcast_to(order[pl.ds(first + n, 1), :], (8, LANES))
            for k in range(4):
                ordered[n, k] = pick(fields, offset + k, index)
            return c

        lax.fori_loop(0, 4, order_block, 0, unroll=4)
        for t in range(2):
            pack_pair(
                first // 2 + t,
                [ordered[2 * t, k] for k in range(4)],
                [ordered[2 * t + 1, k] for k in range(4)],
                buffer,
            )

    def arrange_direction(i, c):
        arrange(i * 4, 0, send_p)
        return c

    lax.fori_loop(0, 4, arrange_direction, 0)

    pl.semaphore_wait(barrier, DEVICES - 1)

    def post_direction(n, c):
        post(0, send_p, recv_p, (me + n) % DEVICES)
        return c

    lax.fori_loop(1, DEVICES, post_direction, 0)
    recv_p[me] = send_p[me]

    def arrange_local(i, c):
        arrange(i * 4, 4, send_l)
        return c

    lax.fori_loop(0, 4, arrange_local, 0)
    recv_l[me] = send_l[me]

    wait_ring(0, recv_p, ring_r)

    def place_pair(pair, c):
        a, b = unpack_pair(pair, recv_p)
        for h, rows in ((0, a), (1, b)):
            i = 2 * pair + h
            for k in range(4):
                grid[i + 1, 8 * k : 8 * k + 8, :] = rows[k]
            grid[i + 1, LAYERS : LAYERS + 1, :] = lateral[pl.ds(i, 1), :]
        return c

    def halo_start(phase):
        ch = pl.ds(phase * PADDED, PADDED)
        above = (region + REGIONS - 1) % REGIONS * TILES + tile
        below = (region + 1) % REGIONS * TILES + tile
        left = region * TILES + (tile + TILES - 1) % TILES
        right = region * TILES + (tile + 1) % TILES
        pairs = (
            (grid.at[1, ch], grid.at[ROWS + 1, ch], above),
            (grid.at[ROWS, ch], grid.at[0, ch], below),
            (edge.at[phase, 0], side.at[phase, 1], left),
            (edge.at[phase, 1], side.at[phase, 0], right),
        )
        copies = [
            pltpu.make_async_remote_copy(
                src_ref=src, dst_ref=dst,
                send_sem=halo_s.at[phase, n], recv_sem=halo_r.at[phase, n],
                device_id=device, device_id_type=LOGICAL,
            )
            for n, (src, dst, device) in enumerate(pairs)
        ]
        for copy in copies:
            copy.start()
        return copies

    def halo_finish(phase, copies):
        for copy in copies:
            copy.wait()
        ch = slice(phase * PADDED, (phase + 1) * PADDED)

        @pl.when(region == 0)
        def _():
            grid[0, ch, :] = jnp.zeros((PADDED, LANES), F32)

        @pl.when(region == REGIONS - 1)
        def _():
            grid[ROWS + 1, ch, :] = jnp.zeros((PADDED, LANES), F32)

        @pl.when(tile == 0)
        def _():
            side[phase, 0] = jnp.zeros((4, LANES), F32)

        @pl.when(tile == TILES - 1)
        def _():
            side[phase, 1] = jnp.zeros((4, LANES), F32)

    def lateral_row(i, phase, west, east):
        ch = slice(phase * PADDED, (phase + 1) * PADDED)
        here = grid[i + 1, ch, :]
        up, down = grid[i, ch, :], grid[i + 2, ch, :]
        west_of = jnp.where(lane == 0, west, pltpu.roll(here, 1, 1))
        east_of = jnp.where(lane == LANES - 1, east, pltpu.roll(here, LANES - 1, 1))
        if phase == 0:
            own = here[LAYERS : LAYERS + 1]
            for n, (other, factor) in enumerate(
                ((up, 0.5), (down, 0.5), (west_of, 0.25), (east_of, 0.25))
            ):
                coef[i, n : n + 1, :] = factor * (own + other[LAYERS : LAYERS + 1])
        return (
            coef[i, 0:1, :] * (here - up)
            + coef[i, 1:2, :] * (here - down)
            + coef[i, 2:3, :] * (here - west_of)
            + coef[i, 3:4, :] * (here - east_of)
        )

    def side_columns(phase, n, lane_to):
        twice = jnp.concatenate([side[phase, n], side[phase, n]], axis=0)
        both = jnp.where(upper, twice, pltpu.roll(twice, 64, 1))

        def column(i):
            return jnp.concatenate(
                [pltpu.roll(both, (lane_to - (s * 16 + i)) % LANES, 1) for s in range(4)], axis=0
            )

        return column

    def lateral_part(phase, out):
        west, east = side_columns(phase, 0, 0), side_columns(phase, 1, LANES - 1)
        dots = [zero] * 2
        for i in range(ROWS):
            value = lateral_row(i, phase, west(i), east(i))
            out[i] = value
            if phase == 0:
                dots[i % 2] = dots[i % 2] + grid[i + 1, 0:PADDED, :] * value
        return dots[0] + dots[1]

    place_pair(0, 0)
    place_pair(ROWS // 2 - 1, 0)
    for n in range(2):
        edge[0, n] = edge[0, n] + edge_of(lambda i: recv_p[i * 8 + 7 * n], n)
    copies = halo_start(0)

    def post_local(n, c):
        post(3, send_l, recv_l, (me + n) % DEVICES)
        return c

    lax.fori_loop(1, DEVICES, post_local, 0)
    lax.fori_loop(1, ROWS // 2 - 1, place_pair, 0, unroll=3)

    halo_finish(0, copies)
    lateral_sum = lateral_part(0, c_grid)

    curve_part = total(jnp.where(inside, lateral_sum + local_sum, 0.0))
    square_part = total(square_sum)

    def turn_pair(pair):
        rows = []
        for h in range(2):
            row = [c_grid[2 * pair + h, 8 * k : 8 * k + 8, :] for k in range(4)]
            row[3] = jnp.where(
                sublane == 6, curve_part, jnp.where(sublane == 7, square_part, row[3])
            )
            rows.append(row)
        pack_pair(pair, rows[0], rows[1], send_b)

    def send_half(i, carry):
        first = (me // 64 + i) % 2 * 4

        def turn(n, c):
            turn_pair(first + n)
            return c

        lax.fori_loop(0, 4, turn, 0, unroll=4)

        def step(n, c):
            post(1, send_b, recv_b, first * 16 + (me + n) % 64)
            return c

        lax.fori_loop(jnp.where(i == 0, 1, 0), 64, step, 0)
        return carry

    lax.fori_loop(0, 2, send_half, 0)
    recv_b[me] = send_b[me]

    wait_ring(3, recv_l, ring_r)

    def add_image(pair, c):
        a, b = unpack_pair(pair, recv_l)
        for h, rows in ((0, a), (1, b)):
            i = 2 * pair + h
            for k in range(4):
                ch = slice(8 * k, 8 * k + 8)
                grid[i + 1, PADDED + 8 * k : PADDED + 8 * k + 8, :] = rows[k] + c_grid[i, ch, :]
        return c

    lax.fori_loop(0, ROWS // 2, add_image, 0, unroll=4)
    for n in range(2):
        edge[1, n] = edge_of(lambda i: recv_l[i * 8 + 7 * n] + send_b[i * 8 + 7 * n], n)
    copies = halo_start(1)

    run = row_iota((24, LANES))
    shift = jnp.where(run < 8, 0, jnp.where(run < 16, DEVICES - 1, DEVICES // 2))
    owner = (me + shift) & (DEVICES - 1)
    wanted = jnp.where((run & 7) < LINES_DEV, owner * LINES_DEV + (run & 7), -1)
    for block in range(BLOCKS):
        hit = line[block : block + 1, :] == wanted
        onehot[:, block * LANES : (block + 1) * LANES] = jnp.where(hit, 1.0, 0.0)
    extended[...] = jnp.ones_like(extended)
    extended[0:LAYERS, :] = model[...]

    def line_sums(slot, values):
        found = lax.dot_general(
            onehot[...], values, (((1,), (1,)), ((), ())),
            precision=lax.Precision.HIGHEST, preferred_element_type=F32,
        )
        for g in range(3):
            sums_s[g, slot, :, 0:PADDED] = found[8 * g : 8 * g + 8, :]

    sums_s[...] = jnp.zeros_like(sums_s)
    line_sums(0, extended[...])
    line_sums(1, fields[0:PADDED, :])

    inverse[...] = lax.fori_loop(
        0, SOUNDINGS // 16, invert, jnp.zeros((BLOCKS, LANES), jnp.int32)
    )

    halo_finish(1, copies)
    lateral_part(1, d_grid)

    wait_ring(1, recv_b, ring_r)
    wait_ring(0, send_p, ring_s)
    wait_ring(3, send_l, ring_s)
    wait_ring(1, send_b, ring_s)

    def take_pair(pair, carried):
        a, b = unpack_pair(pair, recv_b)
        even = pl.ds(pl.multiple_of(pair * 2 * LANES, LANES), LANES)
        odd = pl.ds(pl.multiple_of(pair * 2 * LANES + LANES, LANES), LANES)
        for k in range(4):
            back[8 * k : 8 * k + 8, even] = a[k]
            back[8 * k : 8 * k + 8, odd] = b[k]
        return carried + a[3] + b[3]

    carried = lax.fori_loop(0, BLOCKS // 2, take_pair, jnp.zeros((8, LANES), F32), unroll=4)
    curve = total(carried[6:7]) * (1.0 / 16)
    square = total(carried[7:8]) * (1.0 / 16)
    step_0 = square / curve

    def second_part(block, sums):
        at = pl.ds(pl.multiple_of(block * LANES, LANES), LANES)
        index = jnp.broadcast_to(inverse[pl.ds(block, 1), :], (8, LANES))
        taken = jnp.concatenate([pick(back, k, index) for k in range(4)], axis=0)
        applied = fields[PADDED:, at] + jnp.where(inside, taken, 0.0)
        r = fields[0:PADDED, at] - step_0 * applied
        resid[:, at] = r
        drop = r - pltpu.roll(r, PADDED - 1, 0)
        predicted = jnp.zeros((GATES, LANES), F32)
        for l in range(LAYERS):
            predicted = predicted + jac[l, :, at].astype(F32) * resid[l : l + 1, at]
        return (
            sums[0] + r * r,
            sums[1] + r * applied,
            sums[2] + vert[:, at] * (drop * drop) + DAMPING * (r * r),
            sums[3] + predicted * predicted,
        )

    r_square, r_image, r_curve, r_gates = lax.fori_loop(
        0, BLOCKS, second_part, (zero, zero, zero, jnp.zeros((GATES, LANES), F32)), unroll=4
    )

    def grid_curve(i, acc):
        r = grid[i + 1, 0:PADDED, :] - step_0 * grid[i + 1, PADDED:, :]
        return acc + r * (c_grid[i] - step_0 * d_grid[i])

    r_lateral = lax.fori_loop(0, ROWS, grid_curve, zero, unroll=4)
    r_curve = jnp.where(inside, r_curve + r_lateral, 0.0)

    def rows_sum(values):
        return jnp.sum(values, axis=0, keepdims=True)

    scalars = jnp.where(
        sublane == 0,
        rows_sum(r_square),
        jnp.where(
            sublane == 1,
            rows_sum(r_image),
            jnp.where(sublane == 2, rows_sum(r_curve) + rows_sum(r_gates), 0.0),
        ),
    )
    scalars = jnp.sum(scalars, axis=1, keepdims=True)
    part = rows_sum(jnp.where(sublane == lane_iota((8, LANES)), scalars, 0.0))
    part_s[0] = part
    part_r[me] = part

    def share(i, carry):
        pltpu.make_async_remote_copy(
            src_ref=part_s.at[0],
            dst_ref=part_r.at[me],
            send_sem=ring_s.at[2],
            recv_sem=ring_r.at[2],
            device_id=place((me + i) % DEVICES),
            device_id_type=LOGICAL,
        ).start()
        return carry

    lax.fori_loop(1, 64, share, 0)
    line_sums(2, resid[...])
    sums_copies = []
    for g, offset in ((1, DEVICES - 1), (2, DEVICES // 2)):
        copy = pltpu.make_async_remote_copy(
            src_ref=sums_s.at[g],
            dst_ref=sums_r.at[g - 1],
            send_sem=sums_ss.at[g - 1],
            recv_sem=sums_rs.at[g - 1],
            device_id=place((me + offset) % DEVICES),
            device_id_type=LOGICAL,
        )
        copy.start()
        sums_copies.append(copy)
    lax.fori_loop(64, DEVICES, share, 0)

    wait_ring(2, part_r, ring_r)
    wait_ring(2, part_r, ring_s)
    for copy in sums_copies:
        copy.wait()

    sums = jnp.sum(part_r[...], axis=0)
    square_1, cross, curve_r = sums[:, 0:1], sums[:, 1:2], sums[:, 2:3]
    beta = square_1 / square
    curve_1 = curve_r + 2.0 * beta * cross + beta * beta * curve
    step_1 = square_1 / curve_1
    weight = step_0 + step_1 * beta
    new_model[...] = (
        model[...] + weight * fields[0:LAYERS, :] + step_1 * resid[0:LAYERS, :]
    )
    sums = [sums_s[0, n] + sums_r[0, n] + sums_r[1, n] for n in range(3)]
    count = sums[0][:, LAYERS : LAYERS + 1]
    means = (sums[0] + weight * sums[1] + step_1 * sums[2]) / count
    profile[...] = means[0:LINES_DEV, 0:LAYERS]


def hand_on(model_in, profile_in, model_out, profile_out):
    model_out[...] = model_in[...]
    profile_out[...] = profile_in[...]


def body(jacobian, misfit, model, vertical_weight, lateral_weight, send_order, line_id):
    vmem = pl.BlockSpec(memory_space=pltpu.VMEM)
    dma = pltpu.SemaphoreType.DMA
    outs = pl.pallas_call(
        kernel,
        out_shape=(
            jax.ShapeDtypeStruct((LAYERS, SOUNDINGS), F32),
            jax.ShapeDtypeStruct((LINES_DEV, LAYERS), F32),
        ),
        in_specs=[pl.BlockSpec(memory_space=pltpu.HBM)] * 8,
        out_specs=(vmem, vmem),
        scratch_shapes=[
            pltpu.VMEM((GATES, SOUNDINGS), F32),
            pltpu.VMEM((LAYERS, SOUNDINGS), F32),
            pltpu.VMEM((LAYERS - 1, SOUNDINGS), F32),
            pltpu.VMEM((ROWS, LANES), F32),
            pltpu.VMEM((BLOCKS, LANES), jnp.int32),
            pltpu.SMEM((SOUNDINGS,), jnp.int32),
            pltpu.VMEM((BLOCKS, LANES), jnp.int32),
            pltpu.VMEM((LAYERS, GATES, SOUNDINGS), jnp.bfloat16),
            pltpu.VMEM((2 * PADDED, SOUNDINGS), F32),
            pltpu.VMEM((PADDED, SOUNDINGS), F32),
            pltpu.VMEM((4, 4, 8, LANES), F32),
            pltpu.VMEM((DEVICES, 4, LANES), F32),
            pltpu.VMEM((DEVICES, 4, LANES), F32),
            pltpu.VMEM((DEVICES, 4, LANES), F32),
            pltpu.VMEM((DEVICES, 4, LANES), F32),
            pltpu.VMEM((ROWS + 2, 2 * PADDED, LANES), F32),
            pltpu.VMEM((ROWS, 8, LANES), F32),
            pltpu.VMEM((ROWS, PADDED, LANES), F32),
            pltpu.VMEM((ROWS, PADDED, LANES), F32),
            pltpu.VMEM((2, 2, 4, LANES), F32),
            pltpu.VMEM((2, 2, 4, LANES), F32),
            pltpu.VMEM((DEVICES, 4, LANES), F32),
            pltpu.VMEM((DEVICES, 4, LANES), F32),
            pltpu.VMEM((PADDED, SOUNDINGS), F32),
            pltpu.VMEM((PADDED, SOUNDINGS), F32),
            pltpu.VMEM((BLOCKS, LANES), jnp.int32),
            pltpu.VMEM((24, SOUNDINGS), F32),
            pltpu.VMEM((PADDED, SOUNDINGS), F32),
            pltpu.VMEM((3, 3, 8, LANES), F32),
            pltpu.VMEM((2, 3, 8, LANES), F32),
            pltpu.VMEM((1, 1, LANES), F32),
            pltpu.VMEM((DEVICES, 1, LANES), F32),
            dma((7,)),
            dma((CHUNKS,)),
            dma((4,)),
            dma((4,)),
            dma((2, 4)),
            dma((2, 4)),
            dma((2,)),
            dma((2,)),
        ],
        compiler_params=pltpu.CompilerParams(
            collective_id=0, has_side_effects=True, vmem_limit_bytes=63 * 1024 * 1024
        ),
    )(
        jacobian.transpose(1, 0, 2),
        misfit,
        model,
        vertical_weight,
        lateral_weight,
        send_order.reshape(BLOCKS, LANES),
        send_order,
        line_id.reshape(BLOCKS, LANES),
    )
    return pl.pallas_call(
        hand_on,
        out_shape=(
            jax.ShapeDtypeStruct((LAYERS, SOUNDINGS), F32),
            jax.ShapeDtypeStruct((LINES_DEV, LAYERS), F32),
        ),
        in_specs=[vmem, vmem],
        out_specs=(vmem, vmem),
    )(*outs)


def solution(mesh):
    in_specs = (
        P(None, None, ("region", "tile")),
        P(None, ("region", "tile")),
        P(None, ("region", "tile")),
        P(None, ("region", "tile")),
        P("region", "tile"),
        P(("region", "tile")),
        P(("region", "tile")),
    )
    out_specs = (P(None, ("region", "tile")), P(("region", "tile"), None))
    return jax.shard_map(body, mesh=mesh, in_specs=in_specs, out_specs=out_specs, check_vma=False)
```

```python
import jax
import jax.numpy as jnp
from jax import lax
from jax.experimental import pallas as pl
from jax.experimental.pallas import tpu as pltpu
from jax.sharding import PartitionSpec as P

LINES_DEV = 4
DAMPING = 0.05
GATES = 40
LAYERS = 30
PADDED = 32
SOUNDINGS = 2048
REGIONS = 4
TILES = 32
DEVICES = REGIONS * TILES
ROWS = 16
LANES = 128
BLOCKS = SOUNDINGS // LANES
CHUNKS = 4
LOGICAL = pl.DeviceIdType.LOGICAL
F32 = jnp.float32


def lane_iota(shape):
    return lax.broadcasted_iota(jnp.int32, shape, 1)


def row_iota(shape):
    return lax.broadcasted_iota(jnp.int32, shape, 0)


def total(values):
    return jnp.sum(values, keepdims=True)


def swap_pieces(parts):
    parts = list(parts)
    piece = lane_iota((8, LANES)) // 16
    for bit in (4, 2, 1):
        low = (piece & bit) == 0
        for first in range(8):
            if first & bit:
                continue
            a, b = parts[first], parts[first + bit]
            b_up = pltpu.roll(b, bit * 16, 1)
            a_down = pltpu.roll(a, LANES - bit * 16, 1)
            parts[first] = jnp.where(low, a, b_up)
            parts[first + bit] = jnp.where(low, a_down, b)
    return parts


def layers_of(group):
    return range(8 * group, min(8 * group + 8, LAYERS))


def fold_layers(terms):
    parts = []
    for term in terms:
        rows = [term[8 * n : 8 * n + 8] for n in range(GATES // 8)]
        while len(rows) > 1:
            rows = [sum(rows[n : n + 2][1:], rows[n]) for n in range(0, len(rows), 2)]
        parts.append(rows[0])
    parts += [jnp.zeros((8, LANES), F32)] * (8 - len(parts))
    row = row_iota((8, LANES))
    for bit in (1, 2, 4):
        low = (row & bit) == 0
        parts = [
            jnp.where(low, a, b) + pltpu.roll(jnp.where(low, b, a), bit, 0)
            for a, b in zip(parts[::2], parts[1::2])
        ]
    return parts[0]


def pick(source, group, index):
    low = index & (LANES - 1)
    high = index // LANES
    out = None
    for q in range(BLOCKS):
        block = source[group * 8 : group * 8 + 8, q * LANES : (q + 1) * LANES]
        taken = jnp.take_along_axis(block, low, axis=1, mode="promise_in_bounds")
        out = taken if out is None else jnp.where(high == q, taken, out)
    return out


def kernel(
    jac_in, misfit_in, model_in, vertical_in, lateral_in, order_in, order_flat, line_in,
    new_model, profile,
    misfit, model, vertical, lateral, order, order_s, line,
    jac, fields, vert, ordered, send_p, recv_p, send_l, recv_l, grid, coef, c_grid, d_grid, edge, side,
    send_b, recv_b, back, resid, inverse, onehot, extended,
    sums_s, sums_r, part_s, part_r,
    in_sem, jac_sem, ring_s, ring_r, halo_s, halo_r, sums_ss, sums_rs,
):
    region = lax.axis_index("region")
    tile = lax.axis_index("tile")
    me = region * TILES + tile

    def place(device):
        return device

    def chunk_copy(chunk):
        columns = pl.ds(chunk * (SOUNDINGS // CHUNKS), SOUNDINGS // CHUNKS)
        return pltpu.make_async_copy(
            jac_in.at[:, :, columns], jac.at[:, :, columns], jac_sem.at[chunk]
        )

    loads = [
        pltpu.make_async_copy(src, dst, in_sem.at[n])
        for n, (src, dst) in enumerate(
            (
                (misfit_in, misfit),
                (vertical_in, vertical),
                (order_in, order),
                (order_flat, order_s),
                (lateral_in, lateral),
                (model_in, model),
                (line_in, line),
            )
        )
    ]
    vert[PADDED - 8 :, :] = jnp.zeros((8, SOUNDINGS), F32)
    chunk_copy(0).start()
    loads[0].start()
    loads[1].start()
    for chunk in range(1, CHUNKS):
        chunk_copy(chunk).start()
    for load in loads[2:]:
        load.start()

    barrier = pltpu.get_barrier_semaphore()

    def greet(i, carry):
        pl.semaphore_signal(
            barrier, inc=1, device_id=place((me + i) % DEVICES), device_id_type=LOGICAL
        )
        return carry

    lax.fori_loop(1, DEVICES, greet, 0, unroll=8)

    loads[0].wait()
    loads[1].wait()

    def local_part(block, sums):
        @pl.when(block % (BLOCKS // CHUNKS) == 0)
        def _():
            chunk_copy(block // (BLOCKS // CHUNKS)).wait()

        at = pl.ds(pl.multiple_of(block * LANES, LANES), LANES)

        gate_rows = misfit[:, at]
        for group in range(PADDED // 8):
            fields[8 * group : 8 * group + 8, at] = fold_layers(
                [jac[l, :, at].astype(F32) * gate_rows for l in layers_of(group)]
            )
        predicted = jnp.zeros((GATES, LANES), F32)
        for l in range(LAYERS):
            predicted = predicted + jac[l, :, at].astype(F32) * fields[l : l + 1, at]
        for group in range(PADDED // 8):
            fields[PADDED + 8 * group : PADDED + 8 * group + 8, at] = fold_layers(
                [jac[l, :, at].astype(F32) * predicted for l in layers_of(group)]
            )
        vert[0 : LAYERS - 1, at] = vertical[:, at]
        p = fields[0:PADDED, at]
        flux = vert[:, at] * (p - pltpu.roll(p, PADDED - 1, 0))
        applied = fields[PADDED:, at] + DAMPING * p + (flux - pltpu.roll(flux, 1, 0))
        fields[PADDED:, at] = applied
        return sums[0] + p * p, sums[1] + p * applied

    zero = jnp.zeros((PADDED, LANES), F32)
    square_sum, local_sum = lax.fori_loop(0, BLOCKS, local_part, (zero, zero))

    for load in loads[2:]:
        load.wait()

    upper = row_iota((8, LANES)) < 4
    sublane = row_iota((8, LANES))
    lane = lane_iota((PADDED, LANES))
    layer = row_iota((PADDED, LANES))
    inside = layer < LAYERS
    quarter_row = row_iota((4, LANES))
    quarter_lane = lane_iota((4, LANES))

    def pack_pair(pair, a, b, buffer):
        parts = [jnp.where(upper, a[k], pltpu.roll(b[k], 4, 0)) for k in range(4)]
        parts += [jnp.where(upper, pltpu.roll(a[k], 4, 0), b[k]) for k in range(4)]
        for j, message in enumerate(swap_pieces(parts)):
            buffer[pair * 16 + j] = message[0:4]
            buffer[pair * 16 + 8 + j] = message[4:8]

    def unpack_pair(pair, buffer):
        parts = swap_pieces(
            [
                jnp.concatenate([buffer[pair * 16 + j], buffer[pair * 16 + 8 + j]], axis=0)
                for j in range(8)
            ]
        )
        a = [jnp.where(upper, parts[k], pltpu.roll(parts[k + 4], 4, 0)) for k in range(4)]
        b = [jnp.where(upper, pltpu.roll(parts[k], 4, 0), parts[k + 4]) for k in range(4)]
        return a, b

    def post(ring, source, target, peer):
        pltpu.make_async_remote_copy(
            src_ref=source.at[peer],
            dst_ref=target.at[me],
            send_sem=ring_s.at[ring],
            recv_sem=ring_r.at[ring],
            device_id=peer,
            device_id_type=LOGICAL,
        ).start()

    def wait_ring(ring, buffer, sem):
        whole = buffer.at[pl.ds(0, DEVICES - 1)]
        pltpu.make_async_copy(whole, whole, sem.at[ring]).wait()

    def edge_of(message, side_of):
        out = jnp.zeros((4, LANES), F32)
        for i in range(ROWS):
            moved = pltpu.roll(message(i), (i - 15 * side_of) % LANES, 1)
            out = jnp.where(quarter_lane % 16 == i, moved, out)
        return out

    def weight_edge(side_of):
        out = jnp.zeros((4, LANES), F32)
        for i in range(ROWS):
            moved = jnp.broadcast_to(lateral[i : i + 1, :], (4, LANES))
            moved = pltpu.roll(moved, (112 + i + side_of) % LANES, 1)
            out = jnp.where((quarter_lane == 112 + i) & (quarter_row == 2), moved, out)
        return out

    edge[0, 0] = weight_edge(0)
    edge[0, 1] = weight_edge(1)

    places = row_iota((BLOCKS, LANES)) * LANES + lane_iota((BLOCKS, LANES))

    def invert(first, found):
        for q in range(16):
            found = jnp.where(places == order_s[first * 16 + q], first * 16 + q, found)
        return found

    def arrange(first, offset, buffer):
        def order_block(n, c):
            index = jnp.broadcast_to(order[pl.ds(first + n, 1), :], (8, LANES))
            for k in range(4):
                ordered[n, k] = pick(fields, offset + k, index)
            return c

        lax.fori_loop(0, 4, order_block, 0, unroll=4)
        for t in range(2):
            pack_pair(
                first // 2 + t,
                [ordered[2 * t, k] for k in range(4)],
                [ordered[2 * t + 1, k] for k in range(4)],
                buffer,
            )

    def arrange_direction(i, c):
        arrange(i * 4, 0, send_p)
        return c

    lax.fori_loop(0, 4, arrange_direction, 0)

    pl.semaphore_wait(barrier, DEVICES - 1)

    def post_direction(n, c):
        post(0, send_p, recv_p, (me + n) % DEVICES)
        return c

    lax.fori_loop(1, DEVICES, post_direction, 0, unroll=8)
    recv_p[me] = send_p[me]

    def arrange_local(i, c):
        arrange(i * 4, 4, send_l)
        return c

    lax.fori_loop(0, 4, arrange_local, 0)
    recv_l[me] = send_l[me]

    wait_ring(0, recv_p, ring_r)

    def place_pair(pair, c):
        a, b = unpack_pair(pair, recv_p)
        for h, rows in ((0, a), (1, b)):
            i = 2 * pair + h
            for k in range(4):
                grid[i + 1, 8 * k : 8 * k + 8, :] = rows[k]
            grid[i + 1, LAYERS : LAYERS + 1, :] = lateral[pl.ds(i, 1), :]
        return c

    def halo_start(phase):
        ch = pl.ds(phase * PADDED, PADDED)
        above = (region + REGIONS - 1) % REGIONS * TILES + tile
        below = (region + 1) % REGIONS * TILES + tile
        left = region * TILES + (tile + TILES - 1) % TILES
        right = region * TILES + (tile + 1) % TILES
        pairs = (
            (grid.at[1, ch], grid.at[ROWS + 1, ch], above),
            (grid.at[ROWS, ch], grid.at[0, ch], below),
            (edge.at[phase, 0], side.at[phase, 1], left),
            (edge.at[phase, 1], side.at[phase, 0], right),
        )
        copies = [
            pltpu.make_async_remote_copy(
                src_ref=src, dst_ref=dst,
                send_sem=halo_s.at[phase, n], recv_sem=halo_r.at[phase, n],
                device_id=device, device_id_type=LOGICAL,
            )
            for n, (src, dst, device) in enumerate(pairs)
        ]
        for copy in copies:
            copy.start()
        return copies

    def halo_finish(phase, copies):
        for copy in copies:
            copy.wait()
        ch = slice(phase * PADDED, (phase + 1) * PADDED)

        @pl.when(region == 0)
        def _():
            grid[0, ch, :] = jnp.zeros((PADDED, LANES), F32)

        @pl.when(region == REGIONS - 1)
        def _():
            grid[ROWS + 1, ch, :] = jnp.zeros((PADDED, LANES), F32)

        @pl.when(tile == 0)
        def _():
            side[phase, 0] = jnp.zeros((4, LANES), F32)

        @pl.when(tile == TILES - 1)
        def _():
            side[phase, 1] = jnp.zeros((4, LANES), F32)

    def lateral_row(i, phase, west, east):
        ch = slice(phase * PADDED, (phase + 1) * PADDED)
        here = grid[i + 1, ch, :]
        up, down = grid[i, ch, :], grid[i + 2, ch, :]
        west_of = jnp.where(lane == 0, west, pltpu.roll(here, 1, 1))
        east_of = jnp.where(lane == LANES - 1, east, pltpu.roll(here, LANES - 1, 1))
        if phase == 0:
            own = here[LAYERS : LAYERS + 1]
            for n, (other, factor) in enumerate(
                ((up, 0.5), (down, 0.5), (west_of, 0.25), (east_of, 0.25))
            ):
                coef[i, n : n + 1, :] = factor * (own + other[LAYERS : LAYERS + 1])
        return (
            coef[i, 0:1, :] * (here - up)
            + coef[i, 1:2, :] * (here - down)
            + coef[i, 2:3, :] * (here - west_of)
            + coef[i, 3:4, :] * (here - east_of)
        )

    def side_columns(phase, n, lane_to):
        twice = jnp.concatenate([side[phase, n], side[phase, n]], axis=0)
        both = jnp.where(upper, twice, pltpu.roll(twice, 64, 1))

        def column(i):
            return jnp.concatenate(
                [pltpu.roll(both, (lane_to - (s * 16 + i)) % LANES, 1) for s in range(4)], axis=0
            )

        return column

    def lateral_part(phase, out):
        west, east = side_columns(phase, 0, 0), side_columns(phase, 1, LANES - 1)
        dots = [zero] * 2
        for i in range(ROWS):
            value = lateral_row(i, phase, west(i), east(i))
            out[i] = value
            if phase == 0:
                dots[i % 2] = dots[i % 2] + grid[i + 1, 0:PADDED, :] * value
        return dots[0] + dots[1]

    place_pair(0, 0)
    place_pair(ROWS // 2 - 1, 0)
    for n in range(2):
        edge[0, n] = edge[0, n] + edge_of(lambda i: recv_p[i * 8 + 7 * n], n)
    copies = halo_start(0)

    def post_local(n, c):
        post(3, send_l, recv_l, (me + n) % DEVICES)
        return c

    lax.fori_loop(1, DEVICES, post_local, 0, unroll=8)
    lax.fori_loop(1, ROWS // 2 - 1, place_pair, 0, unroll=3)

    halo_finish(0, copies)
    lateral_sum = lateral_part(0, c_grid)

    curve_part = total(jnp.where(inside, lateral_sum + local_sum, 0.0))
    square_part = total(square_sum)

    def turn_pair(pair):
        rows = []
        for h in range(2):
            row = [c_grid[2 * pair + h, 8 * k : 8 * k + 8, :] for k in range(4)]
            row[3] = jnp.where(
                sublane == 6, curve_part, jnp.where(sublane == 7, square_part, row[3])
            )
            rows.append(row)
        pack_pair(pair, rows[0], rows[1], send_b)

    def send_half(i, carry):
        first = (me // 64 + i) % 2 * 4

        def turn(n, c):
            turn_pair(first + n)
            return c

        lax.fori_loop(0, 4, turn, 0, unroll=4)

        def step(n, c):
            post(1, send_b, recv_b, first * 16 + (me + n) % 64)
            return c

        lax.fori_loop(jnp.where(i == 0, 1, 0), 64, step, 0)
        return carry

    lax.fori_loop(0, 2, send_half, 0)
    recv_b[me] = send_b[me]

    wait_ring(3, recv_l, ring_r)

    def add_image(pair, c):
        a, b = unpack_pair(pair, recv_l)
        for h, rows in ((0, a), (1, b)):
            i = 2 * pair + h
            for k in range(4):
                ch = slice(8 * k, 8 * k + 8)
                grid[i + 1, PADDED + 8 * k : PADDED + 8 * k + 8, :] = rows[k] + c_grid[i, ch, :]
        return c

    lax.fori_loop(0, ROWS // 2, add_image, 0, unroll=4)
    for n in range(2):
        edge[1, n] = edge_of(lambda i: recv_l[i * 8 + 7 * n] + send_b[i * 8 + 7 * n], n)
    copies = halo_start(1)

    run = row_iota((24, LANES))
    shift = jnp.where(run < 8, 0, jnp.where(run < 16, DEVICES - 1, DEVICES // 2))
    owner = (me + shift) & (DEVICES - 1)
    wanted = jnp.where((run & 7) < LINES_DEV, owner * LINES_DEV + (run & 7), -1)
    for block in range(BLOCKS):
        hit = line[block : block + 1, :] == wanted
        onehot[:, block * LANES : (block + 1) * LANES] = jnp.where(hit, 1.0, 0.0)
    extended[...] = jnp.ones_like(extended)
    extended[0:LAYERS, :] = model[...]

    def line_sums(slot, values):
        found = lax.dot_general(
            onehot[...], values, (((1,), (1,)), ((), ())),
            precision=lax.Precision.HIGHEST, preferred_element_type=F32,
        )
        for g in range(3):
            sums_s[g, slot, :, 0:PADDED] = found[8 * g : 8 * g + 8, :]

    sums_s[...] = jnp.zeros_like(sums_s)
    line_sums(0, extended[...])
    line_sums(1, fields[0:PADDED, :])

    inverse[...] = lax.fori_loop(
        0, SOUNDINGS // 16, invert, jnp.zeros((BLOCKS, LANES), jnp.int32)
    )

    halo_finish(1, copies)
    lateral_part(1, d_grid)

    wait_ring(1, recv_b, ring_r)
    wait_ring(0, send_p, ring_s)
    wait_ring(3, send_l, ring_s)
    wait_ring(1, send_b, ring_s)

    def take_pair(pair, carried):
        a, b = unpack_pair(pair, recv_b)
        even = pl.ds(pl.multiple_of(pair * 2 * LANES, LANES), LANES)
        odd = pl.ds(pl.multiple_of(pair * 2 * LANES + LANES, LANES), LANES)
        for k in range(4):
            back[8 * k : 8 * k + 8, even] = a[k]
            back[8 * k : 8 * k + 8, odd] = b[k]
        return carried + a[3] + b[3]

    carried = lax.fori_loop(0, BLOCKS // 2, take_pair, jnp.zeros((8, LANES), F32), unroll=4)
    curve = total(carried[6:7]) * (1.0 / 16)
    square = total(carried[7:8]) * (1.0 / 16)
    step_0 = square / curve

    def second_part(block, sums):
        at = pl.ds(pl.multiple_of(block * LANES, LANES), LANES)
        index = jnp.broadcast_to(inverse[pl.ds(block, 1), :], (8, LANES))
        taken = jnp.concatenate([pick(back, k, index) for k in range(4)], axis=0)
        applied = fields[PADDED:, at] + jnp.where(inside, taken, 0.0)
        r = fields[0:PADDED, at] - step_0 * applied
        resid[:, at] = r
        drop = r - pltpu.roll(r, PADDED - 1, 0)
        predicted = jnp.zeros((GATES, LANES), F32)
        for l in range(LAYERS):
            predicted = predicted + jac[l, :, at].astype(F32) * resid[l : l + 1, at]
        return (
            sums[0] + r * r,
            sums[1] + r * applied,
            sums[2] + vert[:, at] * (drop * drop) + DAMPING * (r * r),
            sums[3] + predicted * predicted,
        )

    r_square, r_image, r_curve, r_gates = lax.fori_loop(
        0, BLOCKS, second_part, (zero, zero, zero, jnp.zeros((GATES, LANES), F32)), unroll=4
    )

    def grid_curve(i, acc):
        r = grid[i + 1, 0:PADDED, :] - step_0 * grid[i + 1, PADDED:, :]
        return acc + r * (c_grid[i] - step_0 * d_grid[i])

    r_lateral = lax.fori_loop(0, ROWS, grid_curve, zero, unroll=4)
    r_curve = jnp.where(inside, r_curve + r_lateral, 0.0)

    def rows_sum(values):
        return jnp.sum(values, axis=0, keepdims=True)

    scalars = jnp.where(
        sublane == 0,
        rows_sum(r_square),
        jnp.where(
            sublane == 1,
            rows_sum(r_image),
            jnp.where(sublane == 2, rows_sum(r_curve) + rows_sum(r_gates), 0.0),
        ),
    )
    scalars = jnp.sum(scalars, axis=1, keepdims=True)
    part = rows_sum(jnp.where(sublane == lane_iota((8, LANES)), scalars, 0.0))
    part_s[0] = part
    part_r[me] = part

    def share(i, carry):
        pltpu.make_async_remote_copy(
            src_ref=part_s.at[0],
            dst_ref=part_r.at[me],
            send_sem=ring_s.at[2],
            recv_sem=ring_r.at[2],
            device_id=place((me + i) % DEVICES),
            device_id_type=LOGICAL,
        ).start()
        return carry

    lax.fori_loop(1, 64, share, 0, unroll=8)
    line_sums(2, resid[...])
    sums_copies = []
    for g, offset in ((1, DEVICES - 1), (2, DEVICES // 2)):
        copy = pltpu.make_async_remote_copy(
            src_ref=sums_s.at[g],
            dst_ref=sums_r.at[g - 1],
            send_sem=sums_ss.at[g - 1],
            recv_sem=sums_rs.at[g - 1],
            device_id=place((me + offset) % DEVICES),
            device_id_type=LOGICAL,
        )
        copy.start()
        sums_copies.append(copy)
    lax.fori_loop(64, DEVICES, share, 0, unroll=8)

    wait_ring(2, part_r, ring_r)
    wait_ring(2, part_r, ring_s)
    for copy in sums_copies:
        copy.wait()

    sums = jnp.sum(part_r[...], axis=0)
    square_1, cross, curve_r = sums[:, 0:1], sums[:, 1:2], sums[:, 2:3]
    beta = square_1 / square
    curve_1 = curve_r + 2.0 * beta * cross + beta * beta * curve
    step_1 = square_1 / curve_1
    weight = step_0 + step_1 * beta
    new_model[...] = (
        model[...] + weight * fields[0:LAYERS, :] + step_1 * resid[0:LAYERS, :]
    )
    sums = [sums_s[0, n] + sums_r[0, n] + sums_r[1, n] for n in range(3)]
    count = sums[0][:, LAYERS : LAYERS + 1]
    means = (sums[0] + weight * sums[1] + step_1 * sums[2]) / count
    profile[...] = means[0:LINES_DEV, 0:LAYERS]


def hand_on(model_in, profile_in, model_out, profile_out):
    model_out[...] = model_in[...]
    profile_out[...] = profile_in[...]


def body(jacobian, misfit, model, vertical_weight, lateral_weight, send_order, line_id):
    vmem = pl.BlockSpec(memory_space=pltpu.VMEM)
    dma = pltpu.SemaphoreType.DMA
    outs = pl.pallas_call(
        kernel,
        out_shape=(
            jax.ShapeDtypeStruct((LAYERS, SOUNDINGS), F32),
            jax.ShapeDtypeStruct((LINES_DEV, LAYERS), F32),
        ),
        in_specs=[pl.BlockSpec(memory_space=pltpu.HBM)] * 8,
        out_specs=(vmem, vmem),
        scratch_shapes=[
            pltpu.VMEM((GATES, SOUNDINGS), F32),
            pltpu.VMEM((LAYERS, SOUNDINGS), F32),
            pltpu.VMEM((LAYERS - 1, SOUNDINGS), F32),
            pltpu.VMEM((ROWS, LANES), F32),
            pltpu.VMEM((BLOCKS, LANES), jnp.int32),
            pltpu.SMEM((SOUNDINGS,), jnp.int32),
            pltpu.VMEM((BLOCKS, LANES), jnp.int32),
            pltpu.VMEM((LAYERS, GATES, SOUNDINGS), jnp.bfloat16),
            pltpu.VMEM((2 * PADDED, SOUNDINGS), F32),
            pltpu.VMEM((PADDED, SOUNDINGS), F32),
            pltpu.VMEM((4, 4, 8, LANES), F32),
            pltpu.VMEM((DEVICES, 4, LANES), F32),
            pltpu.VMEM((DEVICES, 4, LANES), F32),
            pltpu.VMEM((DEVICES, 4, LANES), F32),
            pltpu.VMEM((DEVICES, 4, LANES), F32),
            pltpu.VMEM((ROWS + 2, 2 * PADDED, LANES), F32),
            pltpu.VMEM((ROWS, 8, LANES), F32),
            pltpu.VMEM((ROWS, PADDED, LANES), F32),
            pltpu.VMEM((ROWS, PADDED, LANES), F32),
            pltpu.VMEM((2, 2, 4, LANES), F32),
            pltpu.VMEM((2, 2, 4, LANES), F32),
            pltpu.VMEM((DEVICES, 4, LANES), F32),
            pltpu.VMEM((DEVICES, 4, LANES), F32),
            pltpu.VMEM((PADDED, SOUNDINGS), F32),
            pltpu.VMEM((PADDED, SOUNDINGS), F32),
            pltpu.VMEM((BLOCKS, LANES), jnp.int32),
            pltpu.VMEM((24, SOUNDINGS), F32),
            pltpu.VMEM((PADDED, SOUNDINGS), F32),
            pltpu.VMEM((3, 3, 8, LANES), F32),
            pltpu.VMEM((2, 3, 8, LANES), F32),
            pltpu.VMEM((1, 1, LANES), F32),
            pltpu.VMEM((DEVICES, 1, LANES), F32),
            dma((7,)),
            dma((CHUNKS,)),
            dma((4,)),
            dma((4,)),
            dma((2, 4)),
            dma((2, 4)),
            dma((2,)),
            dma((2,)),
        ],
        compiler_params=pltpu.CompilerParams(
            collective_id=0, has_side_effects=True, vmem_limit_bytes=63 * 1024 * 1024
        ),
    )(
        jacobian.transpose(1, 0, 2),
        misfit,
        model,
        vertical_weight,
        lateral_weight,
        send_order.reshape(BLOCKS, LANES),
        send_order,
        line_id.reshape(BLOCKS, LANES),
    )
    return pl.pallas_call(
        hand_on,
        out_shape=(
            jax.ShapeDtypeStruct((LAYERS, SOUNDINGS), F32),
            jax.ShapeDtypeStruct((LINES_DEV, LAYERS), F32),
        ),
        in_specs=[vmem, vmem],
        out_specs=(vmem, vmem),
    )(*outs)


def solution(mesh):
    in_specs = (
        P(None, None, ("region", "tile")),
        P(None, ("region", "tile")),
        P(None, ("region", "tile")),
        P(None, ("region", "tile")),
        P("region", "tile"),
        P(("region", "tile")),
        P(("region", "tile")),
    )
    out_specs = (P(None, ("region", "tile")), P(("region", "tile"), None))
    return jax.shard_map(body, mesh=mesh, in_specs=in_specs, out_specs=out_specs, check_vma=False)
```

```python
import jax
import jax.numpy as jnp
from jax import lax
from jax.experimental import pallas as pl
from jax.experimental.pallas import tpu as pltpu
from jax.sharding import PartitionSpec as P

LINES_DEV = 4
DAMPING = 0.05
GATES = 40
LAYERS = 30
PADDED = 32
SOUNDINGS = 2048
REGIONS = 4
TILES = 32
DEVICES = REGIONS * TILES
ROWS = 16
LANES = 128
BLOCKS = SOUNDINGS // LANES
CHUNKS = 4
LOGICAL = pl.DeviceIdType.LOGICAL
F32 = jnp.float32


def lane_iota(shape):
    return lax.broadcasted_iota(jnp.int32, shape, 1)


def row_iota(shape):
    return lax.broadcasted_iota(jnp.int32, shape, 0)


def total(values):
    return jnp.sum(values, keepdims=True)


def swap_pieces(parts):
    parts = list(parts)
    piece = lane_iota((8, LANES)) // 16
    for bit in (4, 2, 1):
        low = (piece & bit) == 0
        for first in range(8):
            if first & bit:
                continue
            a, b = parts[first], parts[first + bit]
            b_up = pltpu.roll(b, bit * 16, 1)
            a_down = pltpu.roll(a, LANES - bit * 16, 1)
            parts[first] = jnp.where(low, a, b_up)
            parts[first + bit] = jnp.where(low, a_down, b)
    return parts


def layers_of(group):
    return range(8 * group, min(8 * group + 8, LAYERS))


def fold_layers(terms):
    parts = []
    for term in terms:
        rows = [term[8 * n : 8 * n + 8] for n in range(GATES // 8)]
        while len(rows) > 1:
            rows = [sum(rows[n : n + 2][1:], rows[n]) for n in range(0, len(rows), 2)]
        parts.append(rows[0])
    parts += [jnp.zeros((8, LANES), F32)] * (8 - len(parts))
    row = row_iota((8, LANES))
    for bit in (1, 2, 4):
        low = (row & bit) == 0
        parts = [
            jnp.where(low, a, b) + pltpu.roll(jnp.where(low, b, a), bit, 0)
            for a, b in zip(parts[::2], parts[1::2])
        ]
    return parts[0]


def pick(source, group, index):
    low = index & (LANES - 1)
    high = index // LANES
    out = None
    for q in range(BLOCKS):
        block = source[group * 8 : group * 8 + 8, q * LANES : (q + 1) * LANES]
        taken = jnp.take_along_axis(block, low, axis=1, mode="promise_in_bounds")
        out = taken if out is None else jnp.where(high == q, taken, out)
    return out


def kernel(
    jac_in, misfit_in, model_in, vertical_in, lateral_in, order_in, order_flat, line_in,
    new_model, profile,
    misfit, model, vertical, lateral, order, order_s, line,
    jac, fields, vert, ordered, send_p, recv_p, send_l, recv_l, grid, coef, c_grid, d_grid, edge, side,
    send_b, recv_b, back, resid, inverse, onehot, extended,
    sums_s, sums_r, part_s, part_r,
    in_sem, jac_sem, ring_s, ring_r, halo_s, halo_r, sums_ss, sums_rs,
):
    region = lax.axis_index("region")
    tile = lax.axis_index("tile")
    me = region * TILES + tile

    def place(device):
        return device

    def chunk_copy(chunk):
        columns = pl.ds(chunk * (SOUNDINGS // CHUNKS), SOUNDINGS // CHUNKS)
        return pltpu.make_async_copy(
            jac_in.at[:, :, columns], jac.at[:, :, columns], jac_sem.at[chunk]
        )

    loads = [
        pltpu.make_async_copy(src, dst, in_sem.at[n])
        for n, (src, dst) in enumerate(
            (
                (misfit_in, misfit),
                (vertical_in, vertical),
                (order_in, order),
                (order_flat, order_s),
                (lateral_in, lateral),
                (model_in, model),
                (line_in, line),
            )
        )
    ]
    vert[PADDED - 8 :, :] = jnp.zeros((8, SOUNDINGS), F32)
    chunk_copy(0).start()
    loads[0].start()
    loads[1].start()
    for chunk in range(1, CHUNKS):
        chunk_copy(chunk).start()
    for load in loads[2:]:
        load.start()

    barrier = pltpu.get_barrier_semaphore()

    def greet(i, carry):
        pl.semaphore_signal(
            barrier, inc=1, device_id=place((me + i) % DEVICES), device_id_type=LOGICAL
        )
        return carry

    lax.fori_loop(1, DEVICES, greet, 0, unroll=8)

    loads[0].wait()
    loads[1].wait()

    def local_part(block, sums):
        @pl.when(block % (BLOCKS // CHUNKS) == 0)
        def _():
            chunk_copy(block // (BLOCKS // CHUNKS)).wait()

        at = pl.ds(pl.multiple_of(block * LANES, LANES), LANES)

        gate_rows = misfit[:, at]
        for group in range(PADDED // 8):
            fields[8 * group : 8 * group + 8, at] = fold_layers(
                [jac[l, :, at].astype(F32) * gate_rows for l in layers_of(group)]
            )
        predicted = jnp.zeros((GATES, LANES), F32)
        for l in range(LAYERS):
            predicted = predicted + jac[l, :, at].astype(F32) * fields[l : l + 1, at]
        for group in range(PADDED // 8):
            fields[PADDED + 8 * group : PADDED + 8 * group + 8, at] = fold_layers(
                [jac[l, :, at].astype(F32) * predicted for l in layers_of(group)]
            )
        vert[0 : LAYERS - 1, at] = vertical[:, at]
        p = fields[0:PADDED, at]
        flux = vert[:, at] * (p - pltpu.roll(p, PADDED - 1, 0))
        applied = fields[PADDED:, at] + DAMPING * p + (flux - pltpu.roll(flux, 1, 0))
        fields[PADDED:, at] = applied
        return sums[0] + p * p, sums[1] + p * applied

    zero = jnp.zeros((PADDED, LANES), F32)
    square_sum, local_sum = lax.fori_loop(0, BLOCKS, local_part, (zero, zero))

    for load in loads[2:]:
        load.wait()

    upper = row_iota((8, LANES)) < 4
    sublane = row_iota((8, LANES))
    lane = lane_iota((PADDED, LANES))
    layer = row_iota((PADDED, LANES))
    inside = layer < LAYERS
    quarter_row = row_iota((4, LANES))
    quarter_lane = lane_iota((4, LANES))

    def pack_pair(pair, a, b, buffer):
        parts = [jnp.where(upper, a[k], pltpu.roll(b[k], 4, 0)) for k in range(4)]
        parts += [jnp.where(upper, pltpu.roll(a[k], 4, 0), b[k]) for k in range(4)]
        for j, message in enumerate(swap_pieces(parts)):
            buffer[pair * 16 + j] = message[0:4]
            buffer[pair * 16 + 8 + j] = message[4:8]

    def unpack_pair(pair, buffer):
        parts = swap_pieces(
            [
                jnp.concatenate([buffer[pair * 16 + j], buffer[pair * 16 + 8 + j]], axis=0)
                for j in range(8)
            ]
        )
        a = [jnp.where(upper, parts[k], pltpu.roll(parts[k + 4], 4, 0)) for k in range(4)]
        b = [jnp.where(upper, pltpu.roll(parts[k], 4, 0), parts[k + 4]) for k in range(4)]
        return a, b

    def post(ring, source, target, peer):
        pltpu.make_async_remote_copy(
            src_ref=source.at[peer],
            dst_ref=target.at[me],
            send_sem=ring_s.at[ring],
            recv_sem=ring_r.at[ring],
            device_id=peer,
            device_id_type=LOGICAL,
        ).start()

    def wait_ring(ring, buffer, sem):
        whole = buffer.at[pl.ds(0, DEVICES - 1)]
        pltpu.make_async_copy(whole, whole, sem.at[ring]).wait()

    def edge_of(message, side_of):
        out = jnp.zeros((4, LANES), F32)
        for i in range(ROWS):
            moved = pltpu.roll(message(i), (i - 15 * side_of) % LANES, 1)
            out = jnp.where(quarter_lane % 16 == i, moved, out)
        return out

    def weight_edge(side_of):
        out = jnp.zeros((4, LANES), F32)
        for i in range(ROWS):
            moved = jnp.broadcast_to(lateral[i : i + 1, :], (4, LANES))
            moved = pltpu.roll(moved, (112 + i + side_of) % LANES, 1)
            out = jnp.where((quarter_lane == 112 + i) & (quarter_row == 2), moved, out)
        return out

    edge[0, 0] = weight_edge(0)
    edge[0, 1] = weight_edge(1)

    places = row_iota((BLOCKS, LANES)) * LANES + lane_iota((BLOCKS, LANES))

    def invert(first, found):
        for q in range(16):
            found = jnp.where(places == order_s[first * 16 + q], first * 16 + q, found)
        return found

    def arrange(first, offset, buffer):
        def order_block(n, c):
            index = jnp.broadcast_to(order[pl.ds(first + n, 1), :], (8, LANES))
            for k in range(4):
                ordered[n, k] = pick(fields, offset + k, index)
            return c

        lax.fori_loop(0, 4, order_block, 0, unroll=4)
        for t in range(2):
            pack_pair(
                first // 2 + t,
                [ordered[2 * t, k] for k in range(4)],
                [ordered[2 * t + 1, k] for k in range(4)],
                buffer,
            )

    def arrange_direction(i, c):
        arrange(i * 4, 0, send_p)
        return c

    lax.fori_loop(0, 4, arrange_direction, 0)

    pl.semaphore_wait(barrier, DEVICES - 1)

    def post_direction(n, c):
        post(0, send_p, recv_p, (me + n) % DEVICES)
        return c

    lax.fori_loop(1, DEVICES, post_direction, 0, unroll=8)
    recv_p[me] = send_p[me]

    def arrange_local(i, c):
        arrange(i * 4, 4, send_l)
        return c

    lax.fori_loop(0, 4, arrange_local, 0)
    recv_l[me] = send_l[me]

    def post_local(n, c):
        post(3, send_l, recv_l, (me + n) % DEVICES)
        return c

    lax.fori_loop(1, 65, post_local, 0, unroll=8)

    wait_ring(0, recv_p, ring_r)

    def place_pair(pair, c):
        a, b = unpack_pair(pair, recv_p)
        for h, rows in ((0, a), (1, b)):
            i = 2 * pair + h
            for k in range(4):
                grid[i + 1, 8 * k : 8 * k + 8, :] = rows[k]
            grid[i + 1, LAYERS : LAYERS + 1, :] = lateral[pl.ds(i, 1), :]
        return c

    def halo_start(phase):
        ch = pl.ds(phase * PADDED, PADDED)
        above = (region + REGIONS - 1) % REGIONS * TILES + tile
        below = (region + 1) % REGIONS * TILES + tile
        left = region * TILES + (tile + TILES - 1) % TILES
        right = region * TILES + (tile + 1) % TILES
        pairs = (
            (grid.at[1, ch], grid.at[ROWS + 1, ch], above),
            (grid.at[ROWS, ch], grid.at[0, ch], below),
            (edge.at[phase, 0], side.at[phase, 1], left),
            (edge.at[phase, 1], side.at[phase, 0], right),
        )
        copies = [
            pltpu.make_async_remote_copy(
                src_ref=src, dst_ref=dst,
                send_sem=halo_s.at[phase, n], recv_sem=halo_r.at[phase, n],
                device_id=device, device_id_type=LOGICAL,
            )
            for n, (src, dst, device) in enumerate(pairs)
        ]
        for copy in copies:
            copy.start()
        return copies

    def halo_finish(phase, copies):
        for copy in copies:
            copy.wait()
        ch = slice(phase * PADDED, (phase + 1) * PADDED)

        @pl.when(region == 0)
        def _():
            grid[0, ch, :] = jnp.zeros((PADDED, LANES), F32)

        @pl.when(region == REGIONS - 1)
        def _():
            grid[ROWS + 1, ch, :] = jnp.zeros((PADDED, LANES), F32)

        @pl.when(tile == 0)
        def _():
            side[phase, 0] = jnp.zeros((4, LANES), F32)

        @pl.when(tile == TILES - 1)
        def _():
            side[phase, 1] = jnp.zeros((4, LANES), F32)

    def lateral_row(i, phase, west, east):
        ch = slice(phase * PADDED, (phase + 1) * PADDED)
        here = grid[i + 1, ch, :]
        up, down = grid[i, ch, :], grid[i + 2, ch, :]
        west_of = jnp.where(lane == 0, west, pltpu.roll(here, 1, 1))
        east_of = jnp.where(lane == LANES - 1, east, pltpu.roll(here, LANES - 1, 1))
        if phase == 0:
            own = here[LAYERS : LAYERS + 1]
            for n, (other, factor) in enumerate(
                ((up, 0.5), (down, 0.5), (west_of, 0.25), (east_of, 0.25))
            ):
                coef[i, n : n + 1, :] = factor * (own + other[LAYERS : LAYERS + 1])
        return (
            coef[i, 0:1, :] * (here - up)
            + coef[i, 1:2, :] * (here - down)
            + coef[i, 2:3, :] * (here - west_of)
            + coef[i, 3:4, :] * (here - east_of)
        )

    def side_columns(phase, n, lane_to):
        twice = jnp.concatenate([side[phase, n], side[phase, n]], axis=0)
        both = jnp.where(upper, twice, pltpu.roll(twice, 64, 1))

        def column(i):
            return jnp.concatenate(
                [pltpu.roll(both, (lane_to - (s * 16 + i)) % LANES, 1) for s in range(4)], axis=0
            )

        return column

    def lateral_part(phase, out):
        west, east = side_columns(phase, 0, 0), side_columns(phase, 1, LANES - 1)
        dots = [zero] * 2
        for i in range(ROWS):
            value = lateral_row(i, phase, west(i), east(i))
            out[i] = value
            if phase == 0:
                dots[i % 2] = dots[i % 2] + grid[i + 1, 0:PADDED, :] * value
        return dots[0] + dots[1]

    place_pair(0, 0)
    place_pair(ROWS // 2 - 1, 0)
    for n in range(2):
        edge[0, n] = edge[0, n] + edge_of(lambda i: recv_p[i * 8 + 7 * n], n)
    copies = halo_start(0)

    lax.fori_loop(65, DEVICES, post_local, 0, unroll=8)
    lax.fori_loop(1, ROWS // 2 - 1, place_pair, 0, unroll=3)

    halo_finish(0, copies)
    lateral_sum = lateral_part(0, c_grid)

    curve_part = total(jnp.where(inside, lateral_sum + local_sum, 0.0))
    square_part = total(square_sum)

    def turn_pair(pair):
        rows = []
        for h in range(2):
            row = [c_grid[2 * pair + h, 8 * k : 8 * k + 8, :] for k in range(4)]
            row[3] = jnp.where(
                sublane == 6, curve_part, jnp.where(sublane == 7, square_part, row[3])
            )
            rows.append(row)
        pack_pair(pair, rows[0], rows[1], send_b)

    def send_half(i, carry):
        first = (me // 64 + i) % 2 * 4

        def turn(n, c):
            turn_pair(first + n)
            return c

        lax.fori_loop(0, 4, turn, 0, unroll=4)

        def step(n, c):
            post(1, send_b, recv_b, first * 16 + (me + n) % 64)
            return c

        lax.fori_loop(jnp.where(i == 0, 1, 0), 64, step, 0)
        return carry

    lax.fori_loop(0, 2, send_half, 0)
    recv_b[me] = send_b[me]

    wait_ring(3, recv_l, ring_r)

    def add_image(pair, c):
        a, b = unpack_pair(pair, recv_l)
        for h, rows in ((0, a), (1, b)):
            i = 2 * pair + h
            for k in range(4):
                ch = slice(8 * k, 8 * k + 8)
                grid[i + 1, PADDED + 8 * k : PADDED + 8 * k + 8, :] = rows[k] + c_grid[i, ch, :]
        return c

    lax.fori_loop(0, ROWS // 2, add_image, 0, unroll=4)
    for n in range(2):
        edge[1, n] = edge_of(lambda i: recv_l[i * 8 + 7 * n] + send_b[i * 8 + 7 * n], n)
    copies = halo_start(1)

    run = row_iota((24, LANES))
    shift = jnp.where(run < 8, 0, jnp.where(run < 16, DEVICES - 1, DEVICES // 2))
    owner = (me + shift) & (DEVICES - 1)
    wanted = jnp.where((run & 7) < LINES_DEV, owner * LINES_DEV + (run & 7), -1)
    for block in range(BLOCKS):
        hit = line[block : block + 1, :] == wanted
        onehot[:, block * LANES : (block + 1) * LANES] = jnp.where(hit, 1.0, 0.0)
    extended[...] = jnp.ones_like(extended)
    extended[0:LAYERS, :] = model[...]

    def line_sums(slot, values):
        found = lax.dot_general(
            onehot[...], values, (((1,), (1,)), ((), ())),
            precision=lax.Precision.HIGHEST, preferred_element_type=F32,
        )
        for g in range(3):
            sums_s[g, slot, :, 0:PADDED] = found[8 * g : 8 * g + 8, :]

    sums_s[...] = jnp.zeros_like(sums_s)
    line_sums(0, extended[...])
    line_sums(1, fields[0:PADDED, :])

    inverse[...] = lax.fori_loop(
        0, SOUNDINGS // 16, invert, jnp.zeros((BLOCKS, LANES), jnp.int32)
    )

    halo_finish(1, copies)
    lateral_part(1, d_grid)

    wait_ring(1, recv_b, ring_r)
    wait_ring(0, send_p, ring_s)
    wait_ring(3, send_l, ring_s)
    wait_ring(1, send_b, ring_s)

    def take_pair(pair, carried):
        a, b = unpack_pair(pair, recv_b)
        even = pl.ds(pl.multiple_of(pair * 2 * LANES, LANES), LANES)
        odd = pl.ds(pl.multiple_of(pair * 2 * LANES + LANES, LANES), LANES)
        for k in range(4):
            back[8 * k : 8 * k + 8, even] = a[k]
            back[8 * k : 8 * k + 8, odd] = b[k]
        return carried + a[3] + b[3]

    carried = lax.fori_loop(0, BLOCKS // 2, take_pair, jnp.zeros((8, LANES), F32), unroll=4)
    curve = total(carried[6:7]) * (1.0 / 16)
    square = total(carried[7:8]) * (1.0 / 16)
    step_0 = square / curve

    def second_part(block, sums):
        at = pl.ds(pl.multiple_of(block * LANES, LANES), LANES)
        index = jnp.broadcast_to(inverse[pl.ds(block, 1), :], (8, LANES))
        taken = jnp.concatenate([pick(back, k, index) for k in range(4)], axis=0)
        applied = fields[PADDED:, at] + jnp.where(inside, taken, 0.0)
        r = fields[0:PADDED, at] - step_0 * applied
        resid[:, at] = r
        drop = r - pltpu.roll(r, PADDED - 1, 0)
        predicted = jnp.zeros((GATES, LANES), F32)
        for l in range(LAYERS):
            predicted = predicted + jac[l, :, at].astype(F32) * resid[l : l + 1, at]
        return (
            sums[0] + r * r,
            sums[1] + r * applied,
            sums[2] + vert[:, at] * (drop * drop) + DAMPING * (r * r),
            sums[3] + predicted * predicted,
        )

    r_square, r_image, r_curve, r_gates = lax.fori_loop(
        0, BLOCKS, second_part, (zero, zero, zero, jnp.zeros((GATES, LANES), F32)), unroll=4
    )

    def grid_curve(i, acc):
        r = grid[i + 1, 0:PADDED, :] - step_0 * grid[i + 1, PADDED:, :]
        return acc + r * (c_grid[i] - step_0 * d_grid[i])

    r_lateral = lax.fori_loop(0, ROWS, grid_curve, zero, unroll=4)
    r_curve = jnp.where(inside, r_curve + r_lateral, 0.0)

    def rows_sum(values):
        return jnp.sum(values, axis=0, keepdims=True)

    scalars = jnp.where(
        sublane == 0,
        rows_sum(r_square),
        jnp.where(
            sublane == 1,
            rows_sum(r_image),
            jnp.where(sublane == 2, rows_sum(r_curve) + rows_sum(r_gates), 0.0),
        ),
    )
    scalars = jnp.sum(scalars, axis=1, keepdims=True)
    part = rows_sum(jnp.where(sublane == lane_iota((8, LANES)), scalars, 0.0))
    part_s[0] = part
    part_r[me] = part

    def share(i, carry):
        pltpu.make_async_remote_copy(
            src_ref=part_s.at[0],
            dst_ref=part_r.at[me],
            send_sem=ring_s.at[2],
            recv_sem=ring_r.at[2],
            device_id=place((me + i) % DEVICES),
            device_id_type=LOGICAL,
        ).start()
        return carry

    lax.fori_loop(1, 64, share, 0, unroll=8)
    line_sums(2, resid[...])
    sums_copies = []
    for g, offset in ((1, DEVICES - 1), (2, DEVICES // 2)):
        copy = pltpu.make_async_remote_copy(
            src_ref=sums_s.at[g],
            dst_ref=sums_r.at[g - 1],
            send_sem=sums_ss.at[g - 1],
            recv_sem=sums_rs.at[g - 1],
            device_id=place((me + offset) % DEVICES),
            device_id_type=LOGICAL,
        )
        copy.start()
        sums_copies.append(copy)
    lax.fori_loop(64, DEVICES, share, 0, unroll=8)

    wait_ring(2, part_r, ring_r)
    wait_ring(2, part_r, ring_s)
    for copy in sums_copies:
        copy.wait()

    sums = jnp.sum(part_r[...], axis=0)
    square_1, cross, curve_r = sums[:, 0:1], sums[:, 1:2], sums[:, 2:3]
    beta = square_1 / square
    curve_1 = curve_r + 2.0 * beta * cross + beta * beta * curve
    step_1 = square_1 / curve_1
    weight = step_0 + step_1 * beta
    new_model[...] = (
        model[...] + weight * fields[0:LAYERS, :] + step_1 * resid[0:LAYERS, :]
    )
    sums = [sums_s[0, n] + sums_r[0, n] + sums_r[1, n] for n in range(3)]
    count = sums[0][:, LAYERS : LAYERS + 1]
    means = (sums[0] + weight * sums[1] + step_1 * sums[2]) / count
    profile[...] = means[0:LINES_DEV, 0:LAYERS]


def hand_on(model_in, profile_in, model_out, profile_out):
    model_out[...] = model_in[...]
    profile_out[...] = profile_in[...]


def body(jacobian, misfit, model, vertical_weight, lateral_weight, send_order, line_id):
    vmem = pl.BlockSpec(memory_space=pltpu.VMEM)
    dma = pltpu.SemaphoreType.DMA
    outs = pl.pallas_call(
        kernel,
        out_shape=(
            jax.ShapeDtypeStruct((LAYERS, SOUNDINGS), F32),
            jax.ShapeDtypeStruct((LINES_DEV, LAYERS), F32),
        ),
        in_specs=[pl.BlockSpec(memory_space=pltpu.HBM)] * 8,
        out_specs=(vmem, vmem),
        scratch_shapes=[
            pltpu.VMEM((GATES, SOUNDINGS), F32),
            pltpu.VMEM((LAYERS, SOUNDINGS), F32),
            pltpu.VMEM((LAYERS - 1, SOUNDINGS), F32),
            pltpu.VMEM((ROWS, LANES), F32),
            pltpu.VMEM((BLOCKS, LANES), jnp.int32),
            pltpu.SMEM((SOUNDINGS,), jnp.int32),
            pltpu.VMEM((BLOCKS, LANES), jnp.int32),
            pltpu.VMEM((LAYERS, GATES, SOUNDINGS), jnp.bfloat16),
            pltpu.VMEM((2 * PADDED, SOUNDINGS), F32),
            pltpu.VMEM((PADDED, SOUNDINGS), F32),
            pltpu.VMEM((4, 4, 8, LANES), F32),
            pltpu.VMEM((DEVICES, 4, LANES), F32),
            pltpu.VMEM((DEVICES, 4, LANES), F32),
            pltpu.VMEM((DEVICES, 4, LANES), F32),
            pltpu.VMEM((DEVICES, 4, LANES), F32),
            pltpu.VMEM((ROWS + 2, 2 * PADDED, LANES), F32),
            pltpu.VMEM((ROWS, 8, LANES), F32),
            pltpu.VMEM((ROWS, PADDED, LANES), F32),
            pltpu.VMEM((ROWS, PADDED, LANES), F32),
            pltpu.VMEM((2, 2, 4, LANES), F32),
            pltpu.VMEM((2, 2, 4, LANES), F32),
            pltpu.VMEM((DEVICES, 4, LANES), F32),
            pltpu.VMEM((DEVICES, 4, LANES), F32),
            pltpu.VMEM((PADDED, SOUNDINGS), F32),
            pltpu.VMEM((PADDED, SOUNDINGS), F32),
            pltpu.VMEM((BLOCKS, LANES), jnp.int32),
            pltpu.VMEM((24, SOUNDINGS), F32),
            pltpu.VMEM((PADDED, SOUNDINGS), F32),
            pltpu.VMEM((3, 3, 8, LANES), F32),
            pltpu.VMEM((2, 3, 8, LANES), F32),
            pltpu.VMEM((1, 1, LANES), F32),
            pltpu.VMEM((DEVICES, 1, LANES), F32),
            dma((7,)),
            dma((CHUNKS,)),
            dma((4,)),
            dma((4,)),
            dma((2, 4)),
            dma((2, 4)),
            dma((2,)),
            dma((2,)),
        ],
        compiler_params=pltpu.CompilerParams(
            collective_id=0, has_side_effects=True, vmem_limit_bytes=63 * 1024 * 1024
        ),
    )(
        jacobian.transpose(1, 0, 2),
        misfit,
        model,
        vertical_weight,
        lateral_weight,
        send_order.reshape(BLOCKS, LANES),
        send_order,
        line_id.reshape(BLOCKS, LANES),
    )
    return pl.pallas_call(
        hand_on,
        out_shape=(
            jax.ShapeDtypeStruct((LAYERS, SOUNDINGS), F32),
            jax.ShapeDtypeStruct((LINES_DEV, LAYERS), F32),
        ),
        in_specs=[vmem, vmem],
        out_specs=(vmem, vmem),
    )(*outs)


def solution(mesh):
    in_specs = (
        P(None, None, ("region", "tile")),
        P(None, ("region", "tile")),
        P(None, ("region", "tile")),
        P(None, ("region", "tile")),
        P("region", "tile"),
        P(("region", "tile")),
        P(("region", "tile")),
    )
    out_specs = (P(None, ("region", "tile")), P(("region", "tile"), None))
    return jax.shard_map(body, mesh=mesh, in_specs=in_specs, out_specs=out_specs, check_vma=False)
```
